512 devices in a mesh: group: 64 (over y, z), head: 8 (over x, core).
Axes of the slice: x: 4, y: 8, z: 8, core: 2. Of those that a mesh axis runs over, the one named last changes fastest.
Arguments:
- queries: bfloat16 [1024, 8, 64, 128], P('group', None, 'head'), may hold values from -12 to 12
- fresh_kv: bfloat16 [1024, 8, 8, 2, 128], P('group', None, 'head'), may hold values from -4 to 4
- page_pool: bfloat16 [4096, 8, 2, 128, 128], P('group', 'head'), may hold values from -6 to 6
- context_len: int32 [1024], P('group'), may hold values from 1 to 1024, as said below
- page_holder: int32 [1024, 8], P('group'), may hold values from 0 to 63, as said below
- page_index: int32 [1024, 8], P('group'), may hold values from 0 to 63
- hot_owner: int32 [1], replicated, may hold values from 0 to 63
- hot_pages: int32 [32], replicated, may hold values from 0 to 63
Outputs:
- attended: bfloat16 [1024, 8, 64, 128], P('group', None, 'head')
The draws below stay inside these ranges and needn't reach their ends.
Inputs may be any that keep to these rules, and one draw needn't show every extreme that they name: `context_len`: in each decode group of 16 requests one request has exactly 1024 tokens. `page_holder`: among the entries of one decode group's 16 requests each holder group is named at most 2 times; entries of pages past a request's context are not read.
All inputs are finite; a program needn't handle non-finite values.
Results may differ from the reference program's by a relative error of at most 0.02.
Values may be sent and summed in bfloat16 or wider, within the bound.
No kernel may reach another device: no remote copies, remote signals or barrier semaphores. Data moves between devices by JAX's collectives and lax.ppermute only.
A program may use at most 128 MiB of HBM per device.

```python
import math
import jax
import jax.numpy as jnp
from jax import lax

HD = 128
QH = 64
KVH = 8
PAGE = 128
STEPS = 8
HOTP = 32
MAXP = 8
POOL = 64
REQ = 16
REQS = 1024
CAP = 2
N_GROUP = 64


def draw_queries(key, part):
    key = jax.random.fold_in(key, 11)
    drawn = 2.5 * jax.random.truncated_normal(key, -4.8, 4.8, (REQS, STEPS, QH, HD), jnp.float32)
    return drawn.astype(jnp.bfloat16)


def draw_fresh_kv(key, part):
    key = jax.random.fold_in(key, 23)
    drawn = jax.random.truncated_normal(key, -4.0, 4.0, (REQS, STEPS, KVH, 2, HD), jnp.float32)
    return drawn.astype(jnp.bfloat16)


def draw_context_len(key, part):
    key = jax.random.fold_in(key, 31)
    len_key, pick_key = jax.random.split(key)
    longest = MAXP * PAGE
    drawn = jax.random.randint(len_key, (N_GROUP, REQ), 1, longest + 1)
    longest_at = jax.random.randint(pick_key, (N_GROUP, 1), 0, REQ)
    drawn = jnp.where(jnp.arange(REQ)[None, :] == longest_at, longest, drawn)
    return drawn.reshape(REQS).astype(jnp.int32)


def one_order(group_key):
    return jax.random.permutation(group_key, N_GROUP)


def draw_page_holder(key, part):
    key = jax.random.fold_in(key, 47)
    orders = jax.vmap(one_order)(jax.random.split(key, N_GROUP))
    slot_owner = jnp.arange(REQ * MAXP) // CAP
    holders = orders[:, slot_owner]
    return holders.reshape(REQS, MAXP).astype(jnp.int32)


def place_ends(values, own_key, low, largest):
    longest = values.shape.index(max(values.shape))
    spots = []
    for shift in (0, 1):
        where = [jax.random.randint(jax.random.fold_in(own_key, axis), (), 0, length) for axis, length in enumerate(values.shape)]
        where[longest] = (where[longest] + shift) % values.shape[longest]
        spots.append(tuple(where))
    return values.at[spots[0]].set(low).at[spots[1]].set(largest)


def block_levels(rng, shape, pieces, low, top_value):
    factor_of = 1.0
    for dim, blocks in pieces:
        steps = jax.random.uniform(jax.random.fold_in(jax.random.fold_in(rng, 6), dim), (blocks,), jnp.float32, low / len(pieces), top_value / len(pieces))
        factor_of = factor_of * jnp.repeat(jnp.exp(steps), shape[dim] // blocks).reshape((-1,) + (1,) * (len(shape) - 1 - dim))
    return factor_of


def bell_draw(key, shape, deviation, most, pieces=(), kind=jnp.bfloat16):
    entries = jax.random.normal(key, shape, jnp.float32) * deviation
    if len(pieces) > 0:
        entries = block_levels(key, shape, pieces, -0.22, 0.18) * entries
    return jnp.clip(entries, min=-most, max=most).astype(kind)


def setup_inputs(seed: int = 0) -> dict:
    seeds = jax.random.split(jax.random.key(seed), 9)
    queries = draw_queries(jax.random.fold_in(seeds[8], 71), 0)
    fresh_kv = draw_fresh_kv(jax.random.fold_in(seeds[8], 71), 0)
    page_pool = bell_draw(seeds[2], (N_GROUP * POOL, KVH, 2, PAGE, HD), 1.0, 6.0, ((0, 64), (1, 8)))
    context_len = draw_context_len(jax.random.fold_in(seeds[8], 71), 0)
    page_holder = draw_page_holder(jax.random.fold_in(seeds[8], 71), 0)
    page_index = place_ends(jax.random.randint(seeds[5], (REQS, MAXP), 0, POOL), jax.random.fold_in(seeds[5], 1), 0, POOL - 1).astype(jnp.int32)
    hot_owner = jax.random.randint(seeds[6], (1,), 0, N_GROUP).astype(jnp.int32)
    hot_pages = place_ends(jax.random.randint(seeds[7], (HOTP,), 0, POOL), jax.random.fold_in(seeds[7], 1), 0, POOL - 1).astype(jnp.int32)
    return {"queries": queries, "fresh_kv": fresh_kv, "page_pool": page_pool, "context_len": context_len, "page_holder": page_holder, "page_index": page_index, "hot_owner": hot_owner, "hot_pages": hot_pages}


NEG_FILL = -1e+30

def rounded(weights):
    return lax.optimization_barrier(weights.astype(jnp.bfloat16)).astype(jnp.float32)

def reference(queries, fresh_kv, page_pool, context_len, page_holder, page_index, hot_owner, hot_pages):
    per_kv = QH // KVH
    score_scale = 1.0 / math.sqrt(HD)
    hot_kv = jnp.take(page_pool, hot_owner[0] * POOL + hot_pages, axis=0)
    hot_keys = hot_kv[:, :, 0].astype(jnp.float32)
    hot_values = hot_kv[:, :, 1].astype(jnp.float32)
    page_ids = (page_holder * POOL + page_index).astype(jnp.int32)
    token_order = jnp.arange(MAXP * PAGE, dtype=jnp.int32)
    step_order = jnp.arange(STEPS, dtype=jnp.int32)
    causal = step_order[None, :] <= step_order[:, None]

    def one_group(first_row):
        query_rows = lax.dynamic_slice_in_dim(queries, first_row, REQ, 0).astype(jnp.float32)
        query_rows = query_rows.reshape(REQ, STEPS, KVH, per_kv, HD)
        fresh_rows = lax.dynamic_slice_in_dim(fresh_kv, first_row, REQ, 0).astype(jnp.float32)
        lengths = lax.dynamic_slice_in_dim(context_len, first_row, REQ, 0)
        own_pages = jnp.take(page_pool, lax.dynamic_slice_in_dim(page_ids, first_row, REQ, 0), axis=0)
        private_keys = own_pages[:, :, :, 0].astype(jnp.float32).transpose(0, 2, 1, 3, 4).reshape(REQ, KVH, MAXP * PAGE, HD)
        private_values = own_pages[:, :, :, 1].astype(jnp.float32).transpose(0, 2, 1, 3, 4).reshape(REQ, KVH, MAXP * PAGE, HD)
        hot_scores = jnp.einsum('rsxgd,pxtd->rsxgpt', query_rows, hot_keys).reshape(REQ, STEPS, KVH, per_kv, HOTP * PAGE) * score_scale
        private_scores = jnp.einsum('rsxgd,rxkd->rsxgk', query_rows, private_keys) * score_scale
        fresh_scores = jnp.einsum('rsxgd,rkxd->rsxgk', query_rows, fresh_rows[:, :, :, 0]) * score_scale
        private_mask = (token_order[None, :] < lengths[:, None])[:, None, None, None, :]
        fresh_mask = causal[None, :, None, None, :]
        private_scores = jnp.where(private_mask, private_scores, NEG_FILL)
        fresh_scores = jnp.where(fresh_mask, fresh_scores, NEG_FILL)
        row_max = jnp.maximum(lax.optimization_barrier(jnp.max(hot_scores, axis=4)), jnp.maximum(lax.optimization_barrier(jnp.max(private_scores, axis=4)), lax.optimization_barrier(jnp.max(fresh_scores, axis=4))))
        hot_exp = jnp.exp(hot_scores - row_max[..., None])
        private_exp = jnp.where(private_mask, jnp.exp(private_scores - row_max[..., None]), 0.0)
        fresh_exp = jnp.where(fresh_mask, jnp.exp(fresh_scores - row_max[..., None]), 0.0)
        weight_sum = lax.optimization_barrier(jnp.sum(hot_exp, axis=4)) + lax.optimization_barrier(jnp.sum(private_exp, axis=4)) + lax.optimization_barrier(jnp.sum(fresh_exp, axis=4))
        weighted = jnp.einsum('rsxgpt,pxtd->rsxgd', rounded(hot_exp).reshape(REQ, STEPS, KVH, per_kv, HOTP, PAGE), hot_values)
        weighted = weighted + jnp.einsum('rsxgk,rxkd->rsxgd', rounded(private_exp), private_values)
        weighted = weighted + jnp.einsum('rsxgk,rkxd->rsxgd', rounded(fresh_exp), fresh_rows[:, :, :, 1])
        return (weighted / weight_sum[..., None]).astype(jnp.bfloat16).reshape(REQ, STEPS, QH, HD)
    blocks = lax.map(one_group, jnp.arange(N_GROUP, dtype=jnp.int32) * REQ)
    return blocks.reshape(REQS, STEPS, QH, HD)
```

```python
import functools
import math

import jax
import jax.numpy as jnp
from jax import lax
from jax.experimental import pallas as pl
from jax.experimental.pallas import tpu as pltpu
from jax.sharding import PartitionSpec as P

NEG_FILL = -1e30
CAP = 2
EXTRA = 8
VMEM_LIMIT = 48 * 1024 * 1024

SMEM_SPEC = pl.BlockSpec(memory_space=pltpu.SMEM)
VMEM_SPEC = pl.BlockSpec(memory_space=pltpu.VMEM)


def spread(value, axis, source):
    kept = jnp.where(lax.axis_index(axis) == source, value, 0).astype(value.dtype)
    return lax.psum(kept, axis)


def ask_kernel(len_ref, holder_ref, index_ref, q_ref, ask_ref, slot_ref, count_ref, *, page_len):
    requests, max_pages = holder_ref.shape
    groups = ask_ref.shape[0]
    rows = q_ref.shape[1]
    body = CAP * rows
    lanes = ask_ref.shape[2]

    def clear(g, carry):
        count_ref[g] = 0
        ask_ref[g, pl.ds(body, EXTRA), :] = jnp.zeros((EXTRA, lanes), ask_ref.dtype)
        return carry

    lax.fori_loop(0, groups, clear, 0)
    sub = lax.broadcasted_iota(jnp.int32, (EXTRA, lanes), 0)
    lane = lax.broadcasted_iota(jnp.int32, (EXTRA, lanes), 1)

    def one(i, carry):
        r = i // max_pages
        p = i - r * max_pages
        filled = jnp.clip(len_ref[r] - p * page_len, 0, page_len)
        slot_ref[i] = -1

        @pl.when(filled > 0)
        def _():
            h = holder_ref[r, p]
            rank = jnp.minimum(count_ref[h], CAP - 1)
            count_ref[h] = rank + 1
            slot_ref[i] = h * CAP + rank
            ask_ref[h, pl.ds(pl.multiple_of(rank * rows, rows), rows), :] = q_ref[r]
            page = index_ref[r, p].astype(jnp.float32)
            old = ask_ref[h, pl.ds(body, EXTRA), :].astype(jnp.float32)
            new = jnp.where(lane == 0, page, filled.astype(jnp.float32))
            ask_ref[h, pl.ds(body, EXTRA), :] = jnp.where(
                (sub == rank) & (lane < 2), new, old
            ).astype(ask_ref.dtype)

        return carry

    lax.fori_loop(0, requests * max_pages, one, 0)


def ask(context_len, page_holder, page_index, q, groups, page_len):
    requests, max_pages = page_holder.shape
    rows, lanes = q.shape[1:]
    return pl.pallas_call(
        functools.partial(ask_kernel, page_len=page_len),
        out_shape=(
            jax.ShapeDtypeStruct((groups, CAP * rows + EXTRA, lanes), q.dtype),
            jax.ShapeDtypeStruct((requests * max_pages,), jnp.int32),
        ),
        in_specs=[SMEM_SPEC, SMEM_SPEC, SMEM_SPEC, VMEM_SPEC],
        out_specs=(VMEM_SPEC, SMEM_SPEC),
        scratch_shapes=[pltpu.SMEM((groups,), jnp.int32)],
        compiler_params=pltpu.CompilerParams(vmem_limit_bytes=VMEM_LIMIT),
    )(context_len, page_holder, page_index, q)


def serve_kernel(table_ref, asked_ref, pool_ref, out_ref, *, score_scale):
    block = asked_ref.shape[0]
    lanes = asked_ref.shape[2]
    body = asked_ref.shape[1] - EXTRA
    rows = body // CAP
    page_len = pool_ref.shape[2]
    step = pl.program_id(0)
    token = lax.broadcasted_iota(jnp.int32, (rows, page_len), 1)
    column = lax.broadcasted_iota(jnp.int32, (body, lanes), 1)
    scores = []
    pages = []
    for g in range(block):
        for s in range(CAP):
            at = ((step * block + g) * CAP + s) * 2
            page = jnp.clip(table_ref[at], 0, pool_ref.shape[0] - 1)
            filled = table_ref[at + 1]
            q = asked_ref[g, s * rows : (s + 1) * rows, :]
            keys = pool_ref[page, 0]
            sc = lax.dot_general(
                q, keys, (((1,), (1,)), ((), ())), preferred_element_type=jnp.float32
            )
            scores.append(jnp.where(token < filled, sc * score_scale, NEG_FILL))
            pages.append(page)
    stats = jnp.zeros((body, lanes), jnp.float32)
    for g in range(block):
        both = []
        for s in range(CAP):
            sc = scores[g * CAP + s]
            top = jnp.max(sc, axis=1, keepdims=True)
            ex = jnp.exp(sc - top)
            total = jnp.sum(ex, axis=1, keepdims=True)
            mix = jnp.dot(
                ex.astype(jnp.bfloat16),
                pool_ref[pages[g * CAP + s], 1],
                preferred_element_type=jnp.float32,
            )
            out_ref[g, s * rows : (s + 1) * rows, :] = (mix / total).astype(out_ref.dtype)
            both.append(top + jnp.log(total))
        stats = jnp.where(column == g, jnp.concatenate(both, axis=0), stats)
    flat = stats.T
    high = flat.astype(jnp.bfloat16).astype(jnp.float32)
    low = flat - high
    sub = lax.broadcasted_iota(jnp.int32, (EXTRA, lanes), 0)
    for g in range(block):
        tile = jnp.where(sub == 0, high[g : g + 1], jnp.where(sub == 1, low[g : g + 1], 0.0))
        out_ref[g, body : body + EXTRA, :] = tile.astype(out_ref.dtype)


def serve(table, asked, pool, score_scale, block=8):
    groups, tall, lanes = asked.shape
    n_pages, _, page_len, head_dim = pool.shape
    return pl.pallas_call(
        functools.partial(serve_kernel, score_scale=score_scale),
        out_shape=jax.ShapeDtypeStruct(asked.shape, asked.dtype),
        grid_spec=pltpu.PrefetchScalarGridSpec(
            num_scalar_prefetch=1,
            grid=(groups // block,),
            in_specs=[
                pl.BlockSpec((block, tall, lanes), lambda i, t: (i, 0, 0)),
                pl.BlockSpec((n_pages, 2, page_len, head_dim), lambda i, t: (0, 0, 0, 0)),
            ],
            out_specs=pl.BlockSpec((block, tall, lanes), lambda i, t: (i, 0, 0)),
        ),
        compiler_params=pltpu.CompilerParams(vmem_limit_bytes=VMEM_LIMIT),
    )(table, asked, pool)


def near_kernel(q_ref, fresh_ref, hot_ref, mix_ref, stat_ref, *, score_scale, per_kv, chunk):
    block, rows, lanes = q_ref.shape
    steps = fresh_ref.shape[2]
    tokens = hot_ref.shape[1]
    q = q_ref[...].reshape(block * rows, lanes)
    rhs_t = (((1,), (1,)), ((), ()))
    row_step = lax.broadcasted_iota(jnp.int32, (rows, steps), 0) // per_kv
    key_step = lax.broadcasted_iota(jnp.int32, (rows, steps), 1)
    fresh_scores = []
    for b in range(block):
        sc = lax.dot_general(
            q_ref[b], fresh_ref[b, 0], rhs_t, preferred_element_type=jnp.float32
        )
        fresh_scores.append(jnp.where(key_step <= row_step, sc * score_scale, NEG_FILL))
    fresh_all = jnp.concatenate(fresh_scores, axis=0)
    top = jnp.max(fresh_all, axis=1, keepdims=True)
    ex = jnp.exp(fresh_all - top)
    total = jnp.sum(ex, axis=1, keepdims=True)
    exb = ex.astype(jnp.bfloat16)
    mix = jnp.concatenate(
        [
            jnp.dot(
                exb[b * rows : (b + 1) * rows],
                fresh_ref[b, 1],
                preferred_element_type=jnp.float32,
            )
            for b in range(block)
        ],
        axis=0,
    )
    for c in range(tokens // chunk):
        at = slice(c * chunk, (c + 1) * chunk)
        sc = (
            lax.dot_general(q, hot_ref[0, at, :], rhs_t, preferred_element_type=jnp.float32)
            * score_scale
        )
        new_top = jnp.maximum(top, jnp.max(sc, axis=1, keepdims=True))
        ex = jnp.exp(sc - new_top)
        keep = jnp.exp(top - new_top)
        total = total * keep + jnp.sum(ex, axis=1, keepdims=True)
        mix = mix * keep + jnp.dot(
            ex.astype(jnp.bfloat16), hot_ref[1, at, :], preferred_element_type=jnp.float32
        )
        top = new_top
    mix_ref[...] = (mix / total).reshape(block, rows, lanes)
    lse = top + jnp.log(total)
    stat_ref[...] = jnp.broadcast_to(lse, (block * rows, lanes)).reshape(block, rows, lanes)


def near(q, fresh, hot, score_scale, per_kv, block=2, chunk=1024):
    requests, rows, lanes = q.shape
    steps = fresh.shape[2]
    tokens = hot.shape[1]
    spec = pl.BlockSpec((block, rows, lanes), lambda i: (i, 0, 0))
    return pl.pallas_call(
        functools.partial(near_kernel, score_scale=score_scale, per_kv=per_kv, chunk=chunk),
        out_shape=(
            jax.ShapeDtypeStruct(q.shape, jnp.float32),
            jax.ShapeDtypeStruct(q.shape, jnp.float32),
        ),
        grid=(requests // block,),
        in_specs=[
            spec,
            pl.BlockSpec((block, 2, steps, lanes), lambda i: (i, 0, 0, 0)),
            pl.BlockSpec((2, tokens, lanes), lambda i: (0, 0, 0)),
        ],
        out_specs=(spec, spec),
        compiler_params=pltpu.CompilerParams(vmem_limit_bytes=VMEM_LIMIT),
        cost_estimate=pl.CostEstimate(
            flops=4 * requests * rows * tokens * lanes,
            bytes_accessed=2 * tokens * lanes * 2,
            transcendentals=requests * rows * tokens,
        ),
    )(q, fresh, hot)


def merge_kernel(slot_ref, served_ref, mix_ref, stat_ref, out_ref, lse_ref, *, max_pages):
    groups = served_ref.shape[0]
    requests, rows, lanes = mix_ref.shape
    body = CAP * rows

    def unpack(g, carry):
        tile = served_ref[g, pl.ds(body, EXTRA), :].astype(jnp.float32)
        lse_ref[pl.ds(g, 1), :] = tile[0:1] + tile[1:2]
        return carry

    lax.fori_loop(0, groups, unpack, 0)
    lse_ref[pl.ds(body, body), :] = lse_ref[pl.ds(0, body), :].T
    column = lax.broadcasted_iota(jnp.int32, (rows, lanes), 1)

    def one(r, carry):
        own = stat_ref[r]
        own_top = jnp.max(own, axis=1, keepdims=True)
        tops = []
        for p in range(max_pages):
            slot = slot_ref[r * max_pages + p]
            safe = jnp.maximum(slot, 0)
            h = safe // CAP
            rank = safe - h * CAP
            picked = lse_ref[pl.ds(pl.multiple_of(body + rank * rows, rows), rows), :]
            lse = jnp.sum(jnp.where(column == h, picked, 0.0), axis=1, keepdims=True)
            tops.append(jnp.where(slot >= 0, lse, NEG_FILL))
        top = own_top
        for p in range(max_pages):
            top = jnp.maximum(top, tops[p])
        weight = jnp.exp(own_top - top)
        total = weight
        mix = mix_ref[r] * weight
        for p in range(max_pages):
            slot = slot_ref[r * max_pages + p]
            safe = jnp.maximum(slot, 0)
            h = safe // CAP
            rank = safe - h * CAP
            weight = jnp.exp(tops[p] - top)
            total = total + weight
            part = served_ref[h, pl.ds(pl.multiple_of(rank * rows, rows), rows), :]
            mix = mix + jnp.where(slot >= 0, part.astype(jnp.float32) * weight, 0.0)
        out_ref[r] = (mix / total).astype(out_ref.dtype)
        return carry

    lax.fori_loop(0, requests, one, 0)


def merge(slots, served, mix, stat, max_pages):
    requests, rows, lanes = mix.shape
    return pl.pallas_call(
        functools.partial(merge_kernel, max_pages=max_pages),
        out_shape=jax.ShapeDtypeStruct(mix.shape, jnp.bfloat16),
        in_specs=[SMEM_SPEC, VMEM_SPEC, VMEM_SPEC, VMEM_SPEC],
        out_specs=VMEM_SPEC,
        scratch_shapes=[pltpu.VMEM((2 * CAP * rows, lanes), jnp.float32)],
        compiler_params=pltpu.CompilerParams(vmem_limit_bytes=VMEM_LIMIT),
    )(slots, served, mix, stat)


def on_device(
    queries, fresh_kv, page_pool, context_len, page_holder, page_index, hot_owner, hot_pages
):
    requests, steps, local_heads, head_dim = queries.shape
    page_len = page_pool.shape[3]
    max_pages = page_holder.shape[1]
    groups = lax.axis_size("group")
    score_scale = 1.0 / math.sqrt(head_dim)
    q = queries.reshape(requests, steps * local_heads, head_dim)
    fresh = fresh_kv[:, :, 0].transpose(0, 2, 1, 3)
    pool = page_pool[:, 0]
    hot_local = jnp.take(pool, hot_pages, axis=0, mode="clip")
    hot = spread(hot_local, "group", hot_owner[0])
    hot = hot.transpose(1, 0, 2, 3).reshape(2, -1, head_dim)
    asked, slots = ask(context_len, page_holder, page_index, q, groups, page_len)
    asked = lax.all_to_all(asked, "group", split_axis=0, concat_axis=0, tiled=True)
    body = CAP * steps * local_heads
    table = asked[:, body : body + CAP, 0:2].astype(jnp.int32).reshape(-1)
    served = serve(table, asked, pool, score_scale)
    served = lax.all_to_all(served, "group", split_axis=0, concat_axis=0, tiled=True)
    mix, stat = near(q, fresh, hot, score_scale, local_heads)
    attended = merge(slots, served, mix, stat, max_pages)
    return attended.reshape(requests, steps, local_heads, head_dim)


def solution(mesh):
    placed = (
        P("group", None, "head", None),
        P("group", None, "head", None, None),
        P("group", "head", None, None, None),
        P("group"),
        P("group", None),
        P("group", None),
        P(),
        P(),
    )
    return jax.shard_map(
        on_device,
        mesh=mesh,
        in_specs=placed,
        out_specs=P("group", None, "head", None),
        check_vma=False,
    )
```

```python
import functools
import math

import jax
import jax.numpy as jnp
from jax import lax
from jax.experimental import pallas as pl
from jax.experimental.pallas import tpu as pltpu
from jax.sharding import PartitionSpec as P

NEG_FILL = -1e30
CAP = 2
EXTRA = 8
VMEM_LIMIT = 48 * 1024 * 1024

SMEM_SPEC = pl.BlockSpec(memory_space=pltpu.SMEM)
VMEM_SPEC = pl.BlockSpec(memory_space=pltpu.VMEM)


def pick_kernel(owns_ref, pages_ref, pool_ref, out_ref):
    chunks = out_ref.shape[0]
    page_len = pool_ref.shape[2]
    per_chunk = out_ref.shape[2] // page_len

    @pl.when(owns_ref[0] != 0)
    def _():
        def one(c, carry):
            for p in range(per_chunk):
                page = jnp.clip(pages_ref[c * per_chunk + p], 0, pool_ref.shape[0] - 1)
                out_ref[c, :, p * page_len : (p + 1) * page_len, :] = pool_ref[page]
            return carry

        lax.fori_loop(0, chunks, one, 0)

    @pl.when(owns_ref[0] == 0)
    def _():
        out_ref[...] = jnp.full(out_ref.shape, -jnp.inf, out_ref.dtype)


def pick(owns, hot_pages, pool, chunks):
    n_hot = hot_pages.shape[0]
    _, two, page_len, head_dim = pool.shape
    return pl.pallas_call(
        pick_kernel,
        out_shape=jax.ShapeDtypeStruct(
            (chunks, two, n_hot // chunks * page_len, head_dim), pool.dtype
        ),
        in_specs=[SMEM_SPEC, SMEM_SPEC, VMEM_SPEC],
        out_specs=VMEM_SPEC,
        compiler_params=pltpu.CompilerParams(vmem_limit_bytes=VMEM_LIMIT),
    )(owns, hot_pages, pool)


def ask_kernel(len_ref, holder_ref, index_ref, q_ref, ask_ref, slot_ref, count_ref, *, page_len):
    requests, max_pages = holder_ref.shape
    groups = ask_ref.shape[0]
    rows = q_ref.shape[1]
    body = CAP * rows
    lanes = ask_ref.shape[2]

    def clear(g, carry):
        count_ref[g] = 0
        ask_ref[g, pl.ds(body, EXTRA), :] = jnp.zeros((EXTRA, lanes), ask_ref.dtype)
        return carry

    lax.fori_loop(0, groups, clear, 0)
    sub = lax.broadcasted_iota(jnp.int32, (EXTRA, lanes), 0)
    lane = lax.broadcasted_iota(jnp.int32, (EXTRA, lanes), 1)

    def one(i, carry):
        r = i // max_pages
        p = i - r * max_pages
        filled = jnp.clip(len_ref[r] - p * page_len, 0, page_len)
        slot_ref[i] = -1

        @pl.when(filled > 0)
        def _():
            h = holder_ref[r, p]
            rank = jnp.minimum(count_ref[h], CAP - 1)
            count_ref[h] = rank + 1
            slot_ref[i] = h * CAP + rank
            ask_ref[h, pl.ds(pl.multiple_of(rank * rows, rows), rows), :] = q_ref[r]
            page = index_ref[r, p].astype(jnp.float32)
            old = ask_ref[h, pl.ds(body, EXTRA), :].astype(jnp.float32)
            new = jnp.where(lane == 0, page, filled.astype(jnp.float32))
            ask_ref[h, pl.ds(body, EXTRA), :] = jnp.where(
                (sub == rank) & (lane < 2), new, old
            ).astype(ask_ref.dtype)

        return carry

    lax.fori_loop(0, requests * max_pages, one, 0)


def ask(context_len, page_holder, page_index, q, groups, page_len):
    requests, max_pages = page_holder.shape
    rows, lanes = q.shape[1:]
    return pl.pallas_call(
        functools.partial(ask_kernel, page_len=page_len),
        out_shape=(
            jax.ShapeDtypeStruct((groups, CAP * rows + EXTRA, lanes), q.dtype),
            jax.ShapeDtypeStruct((requests * max_pages,), jnp.int32),
        ),
        in_specs=[SMEM_SPEC, SMEM_SPEC, SMEM_SPEC, VMEM_SPEC],
        out_specs=(VMEM_SPEC, SMEM_SPEC),
        scratch_shapes=[pltpu.SMEM((groups,), jnp.int32)],
        compiler_params=pltpu.CompilerParams(vmem_limit_bytes=VMEM_LIMIT),
    )(context_len, page_holder, page_index, q)


def serve_kernel(table_ref, asked_ref, pool_ref, out_ref, *, score_scale):
    block = asked_ref.shape[0]
    lanes = asked_ref.shape[2]
    body = asked_ref.shape[1] - EXTRA
    rows = body // CAP
    page_len = pool_ref.shape[2]
    step = pl.program_id(0)
    token = lax.broadcasted_iota(jnp.int32, (rows, page_len), 1)
    column = lax.broadcasted_iota(jnp.int32, (body, lanes), 1)
    scores = []
    pages = []
    for g in range(block):
        for s in range(CAP):
            at = ((step * block + g) * CAP + s) * 2
            page = jnp.clip(table_ref[at], 0, pool_ref.shape[0] - 1)
            filled = table_ref[at + 1]
            q = asked_ref[g, s * rows : (s + 1) * rows, :]
            keys = pool_ref[page, 0]
            sc = lax.dot_general(
                q, keys, (((1,), (1,)), ((), ())), preferred_element_type=jnp.float32
            )
            scores.append(jnp.where(token < filled, sc * score_scale, NEG_FILL))
            pages.append(page)
    stats = jnp.zeros((body, lanes), jnp.float32)
    for g in range(block):
        both = []
        for s in range(CAP):
            sc = scores[g * CAP + s]
            top = jnp.max(sc, axis=1, keepdims=True)
            ex = jnp.exp(sc - top)
            total = jnp.sum(ex, axis=1, keepdims=True)
            mix = jnp.dot(
                ex.astype(jnp.bfloat16),
                pool_ref[pages[g * CAP + s], 1],
                preferred_element_type=jnp.float32,
            )
            out_ref[g, s * rows : (s + 1) * rows, :] = (mix / total).astype(out_ref.dtype)
            both.append(top + jnp.log(total))
        stats = jnp.where(column == g, jnp.concatenate(both, axis=0), stats)
    flat = stats.T
    high = flat.astype(jnp.bfloat16).astype(jnp.float32)
    low = flat - high
    sub = lax.broadcasted_iota(jnp.int32, (EXTRA, lanes), 0)
    for g in range(block):
        tile = jnp.where(sub == 0, high[g : g + 1], jnp.where(sub == 1, low[g : g + 1], 0.0))
        out_ref[g, body : body + EXTRA, :] = tile.astype(out_ref.dtype)


def serve(table, asked, pool, score_scale, block=8):
    groups, tall, lanes = asked.shape
    n_pages, _, page_len, head_dim = pool.shape
    return pl.pallas_call(
        functools.partial(serve_kernel, score_scale=score_scale),
        out_shape=jax.ShapeDtypeStruct(asked.shape, asked.dtype),
        grid_spec=pltpu.PrefetchScalarGridSpec(
            num_scalar_prefetch=1,
            grid=(groups // block,),
            in_specs=[
                pl.BlockSpec((block, tall, lanes), lambda i, t: (i, 0, 0)),
                pl.BlockSpec((n_pages, 2, page_len, head_dim), lambda i, t: (0, 0, 0, 0)),
            ],
            out_specs=pl.BlockSpec((block, tall, lanes), lambda i, t: (i, 0, 0)),
        ),
        compiler_params=pltpu.CompilerParams(vmem_limit_bytes=VMEM_LIMIT),
    )(table, asked, pool)


def near_kernel(q_ref, fresh_ref, hot_ref, mix_ref, stat_ref, *, score_scale, per_kv):
    block, rows, lanes = q_ref.shape
    steps = fresh_ref.shape[2]
    chunks = hot_ref.shape[0]
    q = q_ref[...].reshape(block * rows, lanes)
    rhs_t = (((1,), (1,)), ((), ()))
    row_step = lax.broadcasted_iota(jnp.int32, (rows, steps), 0) // per_kv
    key_step = lax.broadcasted_iota(jnp.int32, (rows, steps), 1)
    fresh_scores = []
    for b in range(block):
        sc = lax.dot_general(
            q_ref[b], fresh_ref[b, 0], rhs_t, preferred_element_type=jnp.float32
        )
        fresh_scores.append(jnp.where(key_step <= row_step, sc * score_scale, NEG_FILL))
    fresh_all = jnp.concatenate(fresh_scores, axis=0)
    top = jnp.max(fresh_all, axis=1, keepdims=True)
    ex = jnp.exp(fresh_all - top)
    total = jnp.sum(ex, axis=1, keepdims=True)
    exb = ex.astype(jnp.bfloat16)
    mix = jnp.concatenate(
        [
            jnp.dot(
                exb[b * rows : (b + 1) * rows],
                fresh_ref[b, 1],
                preferred_element_type=jnp.float32,
            )
            for b in range(block)
        ],
        axis=0,
    )
    for c in range(chunks):
        sc = (
            lax.dot_general(q, hot_ref[c, 0], rhs_t, preferred_element_type=jnp.float32)
            * score_scale
        )
        new_top = jnp.maximum(top, jnp.max(sc, axis=1, keepdims=True))
        ex = jnp.exp(sc - new_top)
        keep = jnp.exp(top - new_top)
        total = total * keep + jnp.sum(ex, axis=1, keepdims=True)
        mix = mix * keep + jnp.dot(
            ex.astype(jnp.bfloat16), hot_ref[c, 1], preferred_element_type=jnp.float32
        )
        top = new_top
    mix_ref[...] = (mix / total).reshape(block, rows, lanes)
    lse = top + jnp.log(total)
    stat_ref[...] = jnp.broadcast_to(lse, (block * rows, lanes)).reshape(block, rows, lanes)


def near(q, fresh, hot, score_scale, per_kv, block=2):
    requests, rows, lanes = q.shape
    steps = fresh.shape[2]
    chunks, _, chunk, _ = hot.shape
    tokens = chunks * chunk
    spec = pl.BlockSpec((block, rows, lanes), lambda i: (i, 0, 0))
    return pl.pallas_call(
        functools.partial(near_kernel, score_scale=score_scale, per_kv=per_kv),
        out_shape=(
            jax.ShapeDtypeStruct(q.shape, jnp.float32),
            jax.ShapeDtypeStruct(q.shape, jnp.float32),
        ),
        grid=(requests // block,),
        in_specs=[
            spec,
            pl.BlockSpec((block, 2, steps, lanes), lambda i: (i, 0, 0, 0)),
            pl.BlockSpec((chunks, 2, chunk, lanes), lambda i: (0, 0, 0, 0)),
        ],
        out_specs=(spec, spec),
        compiler_params=pltpu.CompilerParams(vmem_limit_bytes=VMEM_LIMIT),
        cost_estimate=pl.CostEstimate(
            flops=4 * requests * rows * tokens * lanes,
            bytes_accessed=2 * tokens * lanes * 2,
            transcendentals=requests * rows * tokens,
        ),
    )(q, fresh, hot)


def merge_kernel(slot_ref, served_ref, mix_ref, stat_ref, out_ref, lse_ref, *, max_pages):
    groups = served_ref.shape[0]
    requests, rows, lanes = mix_ref.shape
    body = CAP * rows

    def unpack(g, carry):
        tile = served_ref[g, pl.ds(body, EXTRA), :].astype(jnp.float32)
        lse_ref[pl.ds(g, 1), :] = tile[0:1] + tile[1:2]
        return carry

    lax.fori_loop(0, groups, unpack, 0)
    lse_ref[pl.ds(body, body), :] = lse_ref[pl.ds(0, body), :].T
    column = lax.broadcasted_iota(jnp.int32, (rows, lanes), 1)

    def one(r, carry):
        own = stat_ref[r]
        own_top = jnp.max(own, axis=1, keepdims=True)
        tops = []
        for p in range(max_pages):
            slot = slot_ref[r * max_pages + p]
            safe = jnp.maximum(slot, 0)
            h = safe // CAP
            rank = safe - h * CAP
            picked = lse_ref[pl.ds(pl.multiple_of(body + rank * rows, rows), rows), :]
            lse = jnp.sum(jnp.where(column == h, picked, 0.0), axis=1, keepdims=True)
            tops.append(jnp.where(slot >= 0, lse, NEG_FILL))
        top = own_top
        for p in range(max_pages):
            top = jnp.maximum(top, tops[p])
        weight = jnp.exp(own_top - top)
        total = weight
        mix = mix_ref[r] * weight
        for p in range(max_pages):
            slot = slot_ref[r * max_pages + p]
            safe = jnp.maximum(slot, 0)
            h = safe // CAP
            rank = safe - h * CAP
            weight = jnp.exp(tops[p] - top)
            total = total + weight
            part = served_ref[h, pl.ds(pl.multiple_of(rank * rows, rows), rows), :]
            mix = mix + jnp.where(slot >= 0, part.astype(jnp.float32) * weight, 0.0)
        out_ref[r] = (mix / total).astype(out_ref.dtype)
        return carry

    lax.fori_loop(0, requests, one, 0)


def merge(slots, served, mix, stat, max_pages):
    requests, rows, lanes = mix.shape
    return pl.pallas_call(
        functools.partial(merge_kernel, max_pages=max_pages),
        out_shape=jax.ShapeDtypeStruct(mix.shape, jnp.bfloat16),
        in_specs=[SMEM_SPEC, VMEM_SPEC, VMEM_SPEC, VMEM_SPEC],
        out_specs=VMEM_SPEC,
        scratch_shapes=[pltpu.VMEM((2 * CAP * rows, lanes), jnp.float32)],
        compiler_params=pltpu.CompilerParams(vmem_limit_bytes=VMEM_LIMIT),
    )(slots, served, mix, stat)


def on_device(
    queries, fresh_kv, page_pool, context_len, page_holder, page_index, hot_owner, hot_pages
):
    requests, steps, local_heads, head_dim = queries.shape
    page_len = page_pool.shape[3]
    max_pages = page_holder.shape[1]
    groups = lax.axis_size("group")
    score_scale = 1.0 / math.sqrt(head_dim)
    q = queries.reshape(requests, steps * local_heads, head_dim)
    fresh = fresh_kv[:, :, 0].transpose(0, 2, 1, 3)
    pool = page_pool[:, 0]
    owns = (hot_owner == lax.axis_index("group")).astype(jnp.int32)
    kept = pick(owns, hot_pages, pool, 4)
    q, kept = lax.optimization_barrier((q, kept))
    hot = lax.pmax(kept, "group")
    asked, slots = ask(context_len, page_holder, page_index, q, groups, page_len)
    asked = lax.all_to_all(asked, "group", split_axis=0, concat_axis=0, tiled=True)
    body = CAP * steps * local_heads
    table = asked[:, body : body + CAP, 0:2].astype(jnp.int32).reshape(-1)
    served = serve(table, asked, pool, score_scale)
    served = lax.all_to_all(served, "group", split_axis=0, concat_axis=0, tiled=True)
    mix, stat = near(q, fresh, hot, score_scale, local_heads)
    attended = merge(slots, served, mix, stat, max_pages)
    return attended.reshape(requests, steps, local_heads, head_dim)


def solution(mesh):
    placed = (
        P("group", None, "head", None),
        P("group", None, "head", None, None),
        P("group", "head", None, None, None),
        P("group"),
        P("group", None),
        P("group", None),
        P(),
        P(),
    )
    return jax.shard_map(
        on_device,
        mesh=mesh,
        in_specs=placed,
        out_specs=P("group", None, "head", None),
        check_vma=False,
    )
```

```python
import functools
import math

import jax
import jax.numpy as jnp
from jax import lax
from jax.experimental import pallas as pl
from jax.experimental.pallas import tpu as pltpu
from jax.sharding import PartitionSpec as P

NEG_FILL = -1e30
CAP = 2
EXTRA = 8
VMEM_LIMIT = 48 * 1024 * 1024

SMEM_SPEC = pl.BlockSpec(memory_space=pltpu.SMEM)
VMEM_SPEC = pl.BlockSpec(memory_space=pltpu.VMEM)


def deal_kernel(hot_ref, pool_ref, out_ref):
    groups, dealt, _ = out_ref.shape
    page_len = pool_ref.shape[2]
    share = dealt // 2
    per_page = page_len // share

    def one(i, carry):
        page = jnp.clip(hot_ref[i], 0, pool_ref.shape[0] - 1)
        for part in range(per_page):
            for half in range(2):
                out_ref[i * per_page + part, half * share : (half + 1) * share, :] = pool_ref[
                    page, half, part * share : (part + 1) * share, :
                ]
        return carry

    lax.fori_loop(0, hot_ref.shape[0], one, 0)


def deal(hot_pages, pool, groups):
    page_len, head_dim = pool.shape[2:]
    dealt = 2 * page_len * hot_pages.shape[0] // groups
    return pl.pallas_call(
        deal_kernel,
        out_shape=jax.ShapeDtypeStruct((groups, dealt, head_dim), pool.dtype),
        in_specs=[SMEM_SPEC, VMEM_SPEC],
        out_specs=VMEM_SPEC,
        compiler_params=pltpu.CompilerParams(vmem_limit_bytes=VMEM_LIMIT),
    )(hot_pages, pool)


def ask_kernel(len_ref, holder_ref, index_ref, q_ref, ask_ref, slot_ref, count_ref, *, page_len):
    requests, max_pages = holder_ref.shape
    groups = ask_ref.shape[0]
    rows = q_ref.shape[1]
    body = CAP * rows
    lanes = ask_ref.shape[2]

    def clear(g, carry):
        count_ref[g] = 0
        ask_ref[g, pl.ds(body, EXTRA), :] = jnp.zeros((EXTRA, lanes), ask_ref.dtype)
        return carry

    lax.fori_loop(0, groups, clear, 0)
    sub = lax.broadcasted_iota(jnp.int32, (EXTRA, lanes), 0)
    lane = lax.broadcasted_iota(jnp.int32, (EXTRA, lanes), 1)

    def one(i, carry):
        r = i // max_pages
        p = i - r * max_pages
        filled = jnp.clip(len_ref[r] - p * page_len, 0, page_len)
        slot_ref[i] = -1

        @pl.when(filled > 0)
        def _():
            h = holder_ref[r, p]
            rank = jnp.minimum(count_ref[h], CAP - 1)
            count_ref[h] = rank + 1
            slot_ref[i] = h * CAP + rank
            ask_ref[h, pl.ds(pl.multiple_of(rank * rows, rows), rows), :] = q_ref[r]
            page = index_ref[r, p].astype(jnp.float32)
            old = ask_ref[h, pl.ds(body, EXTRA), :].astype(jnp.float32)
            new = jnp.where(lane == 0, page, filled.astype(jnp.float32))
            ask_ref[h, pl.ds(body, EXTRA), :] = jnp.where(
                (sub == rank) & (lane < 2), new, old
            ).astype(ask_ref.dtype)

        return carry

    lax.fori_loop(0, requests * max_pages, one, 0)


def ask(context_len, page_holder, page_index, q, groups, page_len):
    requests, max_pages = page_holder.shape
    rows, lanes = q.shape[1:]
    return pl.pallas_call(
        functools.partial(ask_kernel, page_len=page_len),
        out_shape=(
            jax.ShapeDtypeStruct((groups, CAP * rows + EXTRA, lanes), q.dtype),
            jax.ShapeDtypeStruct((requests * max_pages,), jnp.int32),
        ),
        in_specs=[SMEM_SPEC, SMEM_SPEC, SMEM_SPEC, VMEM_SPEC],
        out_specs=(VMEM_SPEC, SMEM_SPEC),
        scratch_shapes=[pltpu.SMEM((groups,), jnp.int32)],
        compiler_params=pltpu.CompilerParams(vmem_limit_bytes=VMEM_LIMIT),
    )(context_len, page_holder, page_index, q)


def serve_kernel(table_ref, asked_ref, pool_ref, out_ref, *, score_scale):
    block = asked_ref.shape[0]
    lanes = asked_ref.shape[2]
    body = out_ref.shape[1] - EXTRA
    rows = body // CAP
    page_len = pool_ref.shape[2]
    step = pl.program_id(0)
    token = lax.broadcasted_iota(jnp.int32, (rows, page_len), 1)
    column = lax.broadcasted_iota(jnp.int32, (body, lanes), 1)
    scores = []
    pages = []
    for g in range(block):
        for s in range(CAP):
            at = ((step * block + g) * CAP + s) * 2
            page = jnp.clip(table_ref[at], 0, pool_ref.shape[0] - 1)
            filled = table_ref[at + 1]
            q = asked_ref[g, s * rows : (s + 1) * rows, :]
            keys = pool_ref[page, 0]
            sc = lax.dot_general(
                q, keys, (((1,), (1,)), ((), ())), preferred_element_type=jnp.float32
            )
            scores.append(jnp.where(token < filled, sc * score_scale, NEG_FILL))
            pages.append(page)
    stats = jnp.zeros((body, lanes), jnp.float32)
    for g in range(block):
        both = []
        for s in range(CAP):
            sc = scores[g * CAP + s]
            top = jnp.max(sc, axis=1, keepdims=True)
            ex = jnp.exp(sc - top)
            total = jnp.sum(ex, axis=1, keepdims=True)
            mix = jnp.dot(
                ex.astype(jnp.bfloat16),
                pool_ref[pages[g * CAP + s], 1],
                preferred_element_type=jnp.float32,
            )
            out_ref[g, s * rows : (s + 1) * rows, :] = (mix / total).astype(out_ref.dtype)
            both.append(top + jnp.log(total))
        stats = jnp.where(column == g, jnp.concatenate(both, axis=0), stats)
    flat = stats.T
    high = flat.astype(jnp.bfloat16).astype(jnp.float32)
    low = flat - high
    sub = lax.broadcasted_iota(jnp.int32, (EXTRA, lanes), 0)
    for g in range(block):
        tile = jnp.where(sub == 0, high[g : g + 1], jnp.where(sub == 1, low[g : g + 1], 0.0))
        out_ref[g, body : body + EXTRA, :] = tile.astype(out_ref.dtype)


def serve(table, asked, pool, rows, score_scale, block=8):
    groups, tall, lanes = asked.shape
    back = CAP * rows + EXTRA
    n_pages, _, page_len, head_dim = pool.shape
    return pl.pallas_call(
        functools.partial(serve_kernel, score_scale=score_scale),
        out_shape=jax.ShapeDtypeStruct((groups, back, lanes), asked.dtype),
        grid_spec=pltpu.PrefetchScalarGridSpec(
            num_scalar_prefetch=1,
            grid=(groups // block,),
            in_specs=[
                pl.BlockSpec((block, tall, lanes), lambda i, t: (i, 0, 0)),
                pl.BlockSpec((n_pages, 2, page_len, head_dim), lambda i, t: (0, 0, 0, 0)),
            ],
            out_specs=pl.BlockSpec((block, back, lanes), lambda i, t: (i, 0, 0)),
        ),
        compiler_params=pltpu.CompilerParams(vmem_limit_bytes=VMEM_LIMIT),
    )(table, asked, pool)


def near_kernel(q_ref, fresh_ref, hot_ref, mix_ref, stat_ref, kv_ref, *, score_scale, per_kv):
    block, rows, lanes = q_ref.shape
    steps = fresh_ref.shape[2]
    shares, _, share, _ = hot_ref.shape
    chunks, _, chunk, _ = kv_ref.shape
    per_chunk = shares // chunks

    @pl.when(pl.program_id(0) == 0)
    def _():
        def lay(c, carry):
            for i in range(per_chunk):
                kv_ref[c, :, i * share : (i + 1) * share, :] = hot_ref[c * per_chunk + i]
            return carry

        lax.fori_loop(0, chunks, lay, 0)

    q = q_ref[...].reshape(block * rows, lanes)
    rhs_t = (((1,), (1,)), ((), ()))
    row_step = lax.broadcasted_iota(jnp.int32, (rows, steps), 0) // per_kv
    key_step = lax.broadcasted_iota(jnp.int32, (rows, steps), 1)
    fresh_scores = []
    for b in range(block):
        sc = lax.dot_general(
            q_ref[b], fresh_ref[b, 0], rhs_t, preferred_element_type=jnp.float32
        )
        fresh_scores.append(jnp.where(key_step <= row_step, sc * score_scale, NEG_FILL))
    fresh_all = jnp.concatenate(fresh_scores, axis=0)
    top = jnp.max(fresh_all, axis=1, keepdims=True)
    ex = jnp.exp(fresh_all - top)
    total = jnp.sum(ex, axis=1, keepdims=True)
    exb = ex.astype(jnp.bfloat16)
    mix = jnp.concatenate(
        [
            jnp.dot(
                exb[b * rows : (b + 1) * rows],
                fresh_ref[b, 1],
                preferred_element_type=jnp.float32,
            )
            for b in range(block)
        ],
        axis=0,
    )
    for c in range(chunks):
        sc = (
            lax.dot_general(q, kv_ref[c, 0], rhs_t, preferred_element_type=jnp.float32)
            * score_scale
        )
        new_top = jnp.maximum(top, jnp.max(sc, axis=1, keepdims=True))
        ex = jnp.exp(sc - new_top)
        keep = jnp.exp(top - new_top)
        total = total * keep + jnp.sum(ex, axis=1, keepdims=True)
        mix = mix * keep + jnp.dot(
            ex.astype(jnp.bfloat16), kv_ref[c, 1], preferred_element_type=jnp.float32
        )
        top = new_top
    mix_ref[...] = (mix / total).reshape(block, rows, lanes)
    lse = top + jnp.log(total)
    stat_ref[...] = jnp.broadcast_to(lse, (block * rows, lanes)).reshape(block, rows, lanes)


def near(q, fresh, hot, score_scale, per_kv, block=2, chunks=4):
    requests, rows, lanes = q.shape
    steps = fresh.shape[2]
    shares, _, share, _ = hot.shape
    tokens = shares * share
    spec = pl.BlockSpec((block, rows, lanes), lambda i: (i, 0, 0))
    return pl.pallas_call(
        functools.partial(near_kernel, score_scale=score_scale, per_kv=per_kv),
        out_shape=(
            jax.ShapeDtypeStruct(q.shape, jnp.float32),
            jax.ShapeDtypeStruct(q.shape, jnp.float32),
        ),
        grid=(requests // block,),
        in_specs=[
            spec,
            pl.BlockSpec((block, 2, steps, lanes), lambda i: (i, 0, 0, 0)),
            pl.BlockSpec((shares, 2, share, lanes), lambda i: (0, 0, 0, 0)),
        ],
        out_specs=(spec, spec),
        scratch_shapes=[pltpu.VMEM((chunks, 2, tokens // chunks, lanes), hot.dtype)],
        compiler_params=pltpu.CompilerParams(vmem_limit_bytes=VMEM_LIMIT),
        cost_estimate=pl.CostEstimate(
            flops=4 * requests * rows * tokens * lanes,
            bytes_accessed=2 * tokens * lanes * 2,
            transcendentals=requests * rows * tokens,
        ),
    )(q, fresh, hot)


def merge_kernel(slot_ref, served_ref, mix_ref, stat_ref, out_ref, lse_ref, *, max_pages):
    groups = served_ref.shape[0]
    requests, rows, lanes = mix_ref.shape
    body = CAP * rows

    def unpack(g, carry):
        tile = served_ref[g, pl.ds(body, EXTRA), :].astype(jnp.float32)
        lse_ref[pl.ds(g, 1), :] = tile[0:1] + tile[1:2]
        return carry

    lax.fori_loop(0, groups, unpack, 0)
    lse_ref[pl.ds(body, body), :] = lse_ref[pl.ds(0, body), :].T
    column = lax.broadcasted_iota(jnp.int32, (rows, lanes), 1)

    def one(r, carry):
        own = stat_ref[r]
        own_top = jnp.max(own, axis=1, keepdims=True)
        tops = []
        for p in range(max_pages):
            slot = slot_ref[r * max_pages + p]
            safe = jnp.maximum(slot, 0)
            h = safe // CAP
            rank = safe - h * CAP
            picked = lse_ref[pl.ds(pl.multiple_of(body + rank * rows, rows), rows), :]
            lse = jnp.sum(jnp.where(column == h, picked, 0.0), axis=1, keepdims=True)
            tops.append(jnp.where(slot >= 0, lse, NEG_FILL))
        top = own_top
        for p in range(max_pages):
            top = jnp.maximum(top, tops[p])
        weight = jnp.exp(own_top - top)
        total = weight
        mix = mix_ref[r] * weight
        for p in range(max_pages):
            slot = slot_ref[r * max_pages + p]
            safe = jnp.maximum(slot, 0)
            h = safe // CAP
            rank = safe - h * CAP
            weight = jnp.exp(tops[p] - top)
            total = total + weight
            part = served_ref[h, pl.ds(pl.multiple_of(rank * rows, rows), rows), :]
            mix = mix + jnp.where(slot >= 0, part.astype(jnp.float32) * weight, 0.0)
        out_ref[r] = (mix / total).astype(out_ref.dtype)
        return carry

    lax.fori_loop(0, requests, one, 0)


def merge(slots, served, mix, stat, max_pages):
    requests, rows, lanes = mix.shape
    return pl.pallas_call(
        functools.partial(merge_kernel, max_pages=max_pages),
        out_shape=jax.ShapeDtypeStruct(mix.shape, jnp.bfloat16),
        in_specs=[SMEM_SPEC, VMEM_SPEC, VMEM_SPEC, VMEM_SPEC],
        out_specs=VMEM_SPEC,
        scratch_shapes=[pltpu.VMEM((2 * CAP * rows, lanes), jnp.float32)],
        compiler_params=pltpu.CompilerParams(vmem_limit_bytes=VMEM_LIMIT),
    )(slots, served, mix, stat)


def exchange(value):
    return lax.all_to_all(value, "group", split_axis=0, concat_axis=0, tiled=True)


def on_device(
    queries, fresh_kv, page_pool, context_len, page_holder, page_index, hot_owner, hot_pages
):
    requests, steps, local_heads, head_dim = queries.shape
    max_pages = page_holder.shape[1]
    groups = lax.axis_size("group")
    score_scale = 1.0 / math.sqrt(head_dim)
    q = queries.reshape(requests, steps * local_heads, head_dim)
    fresh = fresh_kv[:, :, 0].transpose(0, 2, 1, 3)
    pool = page_pool[:, 0]
    rows = steps * local_heads
    body = CAP * rows
    rows = steps * local_heads
    body = CAP * rows
    dealt = exchange(deal(hot_pages, pool, groups))
    asked, slots = ask(
        context_len, page_holder, page_index, q, groups, page_pool.shape[3]
    )
    asked, dealt = lax.optimization_barrier((asked, dealt))
    asked = exchange(asked)
    share = lax.dynamic_index_in_dim(dealt, hot_owner[0], 0, keepdims=False)
    share = jnp.broadcast_to(share, (groups,) + share.shape)
    asked, share = lax.optimization_barrier((asked, share))
    hot = exchange(share)
    table = asked[:, body : body + CAP, 0:2].astype(jnp.int32).reshape(-1)
    served = serve(table, asked, pool, rows, score_scale)
    served, hot = lax.optimization_barrier((served, hot))
    served = exchange(served)
    hot = hot.reshape(groups, 2, -1, head_dim)
    mix, stat = near(q, fresh, hot, score_scale, local_heads)
    attended = merge(slots, served, mix, stat, max_pages)
    return attended.reshape(requests, steps, local_heads, head_dim)


def solution(mesh):
    placed = (
        P("group", None, "head", None),
        P("group", None, "head", None, None),
        P("group", "head", None, None, None),
        P("group"),
        P("group", None),
        P("group", None),
        P(),
        P(),
    )
    return jax.shard_map(
        on_device,
        mesh=mesh,
        in_specs=placed,
        out_specs=P("group", None, "head", None),
        check_vma=False,
    )
```

```python
import functools
import math

import jax
import jax.numpy as jnp
from jax import lax
from jax.experimental import pallas as pl
from jax.experimental.pallas import tpu as pltpu
from jax.sharding import PartitionSpec as P

NEG_FILL = -1e30
CAP = 2
EXTRA = 8
NEAR_WEIGHT = 64
MERGE_BLOCK = 2
VMEM_LIMIT = 48 * 1024 * 1024

SMEM_SPEC = pl.BlockSpec(memory_space=pltpu.SMEM)
VMEM_SPEC = pl.BlockSpec(memory_space=pltpu.VMEM)


def deal_kernel(hot_ref, pool_ref, out_ref):
    def one(i, carry):
        page = jnp.clip(hot_ref[i], 0, pool_ref.shape[0] - 1)
        for part in range(2):
            out_ref[2 * i + part] = pool_ref[page, part]
        return carry

    lax.fori_loop(0, hot_ref.shape[0], one, 0)


def deal(hot_pages, pool):
    _, two, page_len, head_dim = pool.shape
    return pl.pallas_call(
        deal_kernel,
        out_shape=jax.ShapeDtypeStruct((two * hot_pages.shape[0], page_len, head_dim), pool.dtype),
        in_specs=[SMEM_SPEC, VMEM_SPEC],
        out_specs=VMEM_SPEC,
        compiler_params=pltpu.CompilerParams(vmem_limit_bytes=VMEM_LIMIT),
    )(hot_pages, pool)


def ask_kernel(len_ref, holder_ref, index_ref, q_ref, ask_ref, slot_ref, count_ref, *, page_len):
    requests, max_pages = holder_ref.shape
    groups = ask_ref.shape[0]
    rows = q_ref.shape[1]
    body = CAP * rows
    lanes = ask_ref.shape[2]

    def clear(g, carry):
        count_ref[g] = 0
        ask_ref[g, pl.ds(body, EXTRA), :] = jnp.zeros((EXTRA, lanes), ask_ref.dtype)
        return carry

    lax.fori_loop(0, groups, clear, 0)
    sub = lax.broadcasted_iota(jnp.int32, (EXTRA, lanes), 0)
    lane = lax.broadcasted_iota(jnp.int32, (EXTRA, lanes), 1)

    def one(i, carry):
        r = i // max_pages
        p = i - r * max_pages
        filled = jnp.clip(len_ref[r] - p * page_len, 0, page_len)
        slot_ref[i] = -1

        @pl.when(filled > 0)
        def _():
            h = holder_ref[r, p]
            rank = jnp.minimum(count_ref[h], CAP - 1)
            count_ref[h] = rank + 1
            slot_ref[i] = h * CAP + rank
            ask_ref[h, pl.ds(pl.multiple_of(rank * rows, rows), rows), :] = q_ref[r]
            page = index_ref[r, p].astype(jnp.float32)
            old = ask_ref[h, pl.ds(body, EXTRA), :].astype(jnp.float32)
            new = jnp.where(lane == 0, page, filled.astype(jnp.float32))
            ask_ref[h, pl.ds(body, EXTRA), :] = jnp.where(
                (sub == rank) & (lane < 2), new, old
            ).astype(ask_ref.dtype)

        return carry

    lax.fori_loop(0, requests * max_pages, one, 0)


def ask(context_len, page_holder, page_index, q, groups, page_len):
    requests, max_pages = page_holder.shape
    rows, lanes = q.shape[1:]
    return pl.pallas_call(
        functools.partial(ask_kernel, page_len=page_len),
        out_shape=(
            jax.ShapeDtypeStruct((groups, CAP * rows + EXTRA, lanes), q.dtype),
            jax.ShapeDtypeStruct((requests * max_pages,), jnp.int32),
        ),
        in_specs=[SMEM_SPEC, SMEM_SPEC, SMEM_SPEC, VMEM_SPEC],
        out_specs=(VMEM_SPEC, SMEM_SPEC),
        scratch_shapes=[pltpu.SMEM((groups,), jnp.int32)],
        compiler_params=pltpu.CompilerParams(vmem_limit_bytes=VMEM_LIMIT),
    )(context_len, page_holder, page_index, q)


def serve_kernel(table_ref, asked_ref, pool_ref, out_ref, *, factor, block):
    groups, tall, lanes = asked_ref.shape
    body = tall - EXTRA
    rows = body // CAP
    page_len = pool_ref.shape[2]
    token = lax.broadcasted_iota(jnp.int32, (rows, page_len), 1)
    column = lax.broadcasted_iota(jnp.int32, (body, lanes), 1)
    sub = lax.broadcasted_iota(jnp.int32, (EXTRA, lanes), 0)

    def one(step, carry):
        scores = []
        pages = []
        for g in range(block):
            for s in range(CAP):
                at = ((step * block + g) * CAP + s) * 2
                page = jnp.clip(table_ref[at], 0, pool_ref.shape[0] - 1)
                sc = lax.dot_general(
                    asked_ref[step * block + g, s * rows : (s + 1) * rows, :],
                    pool_ref[page, 0],
                    (((1,), (1,)), ((), ())),
                    preferred_element_type=jnp.float32,
                )
                scores.append(jnp.where(token < table_ref[at + 1], sc * factor, NEG_FILL))
                pages.append(page)
        stats = jnp.zeros((body, lanes), jnp.float32)
        for g in range(block):
            both = []
            for s in range(CAP):
                sc = scores[g * CAP + s]
                top = jnp.max(sc, axis=1, keepdims=True)
                ex = jnp.exp2(sc - top)
                total = jnp.sum(ex, axis=1, keepdims=True)
                mix = jnp.dot(
                    ex.astype(jnp.bfloat16),
                    pool_ref[pages[g * CAP + s], 1],
                    preferred_element_type=jnp.float32,
                )
                out_ref[step * block + g, s * rows : (s + 1) * rows, :] = (
                    mix * (1.0 / total)
                ).astype(out_ref.dtype)
                both.append(top + jnp.log2(total))
            stats = jnp.where(column == g, jnp.concatenate(both, axis=0), stats)
        flat = stats.T
        high = flat.astype(jnp.bfloat16).astype(jnp.float32)
        low = flat - high
        for g in range(block):
            tile = jnp.where(sub == 0, high[g : g + 1], jnp.where(sub == 1, low[g : g + 1], 0.0))
            out_ref[step * block + g, body : body + EXTRA, :] = tile.astype(out_ref.dtype)
        return carry

    lax.fori_loop(0, groups // block, one, 0)


def serve(table, asked, pool, factor):
    block = math.gcd(asked.shape[0], 16)
    return pl.pallas_call(
        functools.partial(serve_kernel, factor=factor, block=block),
        out_shape=jax.ShapeDtypeStruct(asked.shape, asked.dtype),
        in_specs=[SMEM_SPEC, VMEM_SPEC, VMEM_SPEC],
        out_specs=VMEM_SPEC,
        compiler_params=pltpu.CompilerParams(vmem_limit_bytes=VMEM_LIMIT),
    )(table, asked, pool)


def near_kernel(q_ref, fresh_ref, hot_ref, mix_ref, stat_ref, kv_ref, *, factor, per_kv, block):
    page_len = hot_ref.shape[1]
    chunks, _, chunk, _ = kv_ref.shape
    per_chunk = chunk // page_len

    def lay(c, carry):
        for i in range(per_chunk):
            for part in range(2):
                kv_ref[c, part, i * page_len : (i + 1) * page_len, :] = hot_ref[
                    2 * (c * per_chunk + i) + part
                ]
        return carry

    lax.fori_loop(0, chunks, lay, 0)
    requests, rows, lanes = q_ref.shape
    steps = fresh_ref.shape[2]
    rhs_t = (((1,), (1,)), ((), ()))
    row_step = lax.broadcasted_iota(jnp.int32, (rows, steps), 0) // per_kv
    key_step = lax.broadcasted_iota(jnp.int32, (rows, steps), 1)

    def one(n, carry):
        at = pl.ds(n * block, block)
        own = q_ref[at]
        q = own.reshape(block * rows, lanes)
        fresh_scores = []
        for b in range(block):
            sc = lax.dot_general(
                own[b], fresh_ref[n * block + b, 0], rhs_t, preferred_element_type=jnp.float32
            )
            fresh_scores.append(jnp.where(key_step <= row_step, sc * factor, NEG_FILL))
        sc = jnp.concatenate(fresh_scores, axis=0)
        top = jnp.max(sc, axis=1, keepdims=True)
        ex = jnp.exp2(sc - top)
        total = jnp.sum(ex, axis=1, keepdims=True)
        weights = ex.astype(jnp.bfloat16)
        mix = jnp.concatenate(
            [
                jnp.dot(
                    weights[b * rows : (b + 1) * rows],
                    fresh_ref[n * block + b, 1],
                    preferred_element_type=jnp.float32,
                )
                for b in range(block)
            ],
            axis=0,
        )
        for c in range(chunks):
            sc = lax.dot_general(q, kv_ref[c, 0], rhs_t, preferred_element_type=jnp.float32)
            new_top = jnp.maximum(top, jnp.max(sc, axis=1, keepdims=True) * factor)
            ex = jnp.exp2(sc * factor - new_top)
            keep = jnp.exp2(top - new_top)
            total = total * keep + jnp.sum(ex, axis=1, keepdims=True)
            mix = mix * keep + jnp.dot(
                ex.astype(jnp.bfloat16), kv_ref[c, 1], preferred_element_type=jnp.float32
            )
            top = new_top
        mix_ref[at] = (mix / total).reshape(block, rows, lanes)
        lse = top + jnp.log2(total)
        stat_ref[at] = jnp.broadcast_to(lse, (block * rows, lanes)).reshape(block, rows, lanes)
        return carry

    lax.fori_loop(0, requests // block, one, 0)


def near(q, fresh, hot, factor, per_kv):
    requests, rows, lanes = q.shape
    tokens = hot.shape[0] // 2 * hot.shape[1]
    block = math.gcd(requests, 8)
    chunks = math.gcd(hot.shape[0] // 2, 8)
    return pl.pallas_call(
        functools.partial(near_kernel, factor=factor, per_kv=per_kv, block=block),
        out_shape=(
            jax.ShapeDtypeStruct(q.shape, jnp.float32),
            jax.ShapeDtypeStruct(q.shape, jnp.float32),
        ),
        in_specs=[VMEM_SPEC] * 3,
        out_specs=(VMEM_SPEC, VMEM_SPEC),
        scratch_shapes=[pltpu.VMEM((chunks, 2, tokens // chunks, lanes), hot.dtype)],
        compiler_params=pltpu.CompilerParams(vmem_limit_bytes=VMEM_LIMIT),
        cost_estimate=pl.CostEstimate(
            flops=NEAR_WEIGHT * 4 * requests * rows * tokens * lanes,
            bytes_accessed=2 * tokens * lanes * 2,
            transcendentals=requests * rows * tokens,
        ),
    )(q, fresh, hot)


def merge_kernel(slot_ref, served_ref, mix_ref, stat_ref, out_ref, lse_ref, *, max_pages):
    groups = served_ref.shape[0]
    requests, rows, lanes = mix_ref.shape
    block = math.gcd(requests, MERGE_BLOCK)
    body = CAP * rows

    def unpack(g, carry):
        tile = served_ref[g, pl.ds(body, EXTRA), :].astype(jnp.float32)
        lse_ref[pl.ds(g, 1), :] = tile[0:1] + tile[1:2]
        return carry

    lax.fori_loop(0, groups, unpack, 0)
    lse_ref[pl.ds(body, body), :] = lse_ref[pl.ds(0, body), :].T
    column = lax.broadcasted_iota(jnp.int32, (rows, lanes), 1)

    def one(n, carry):
        for b in range(block):
            merge_one(n * block + b)
        return carry

    def merge_one(r):
        own = stat_ref[r]
        own_top = jnp.max(own, axis=1, keepdims=True)
        tops = []
        for p in range(max_pages):
            slot = slot_ref[r * max_pages + p]
            safe = jnp.maximum(slot, 0)
            h = safe // CAP
            rank = safe - h * CAP
            picked = lse_ref[pl.ds(pl.multiple_of(body + rank * rows, rows), rows), :]
            lse = jnp.sum(jnp.where(column == h, picked, 0.0), axis=1, keepdims=True)
            tops.append(jnp.where(slot >= 0, lse, NEG_FILL))
        top = own_top
        for p in range(max_pages):
            top = jnp.maximum(top, tops[p])
        weight = jnp.exp2(own_top - top)
        total = weight
        mix = mix_ref[r] * weight
        for p in range(max_pages):
            slot = slot_ref[r * max_pages + p]
            safe = jnp.maximum(slot, 0)
            h = safe // CAP
            rank = safe - h * CAP
            weight = jnp.exp2(tops[p] - top)
            total = total + weight
            part = served_ref[h, pl.ds(pl.multiple_of(rank * rows, rows), rows), :]
            mix = mix + jnp.where(slot >= 0, part.astype(jnp.float32) * weight, 0.0)
        out_ref[r] = (mix / total).astype(out_ref.dtype)

    lax.fori_loop(0, requests // block, one, 0)


def merge(slots, served, mix, stat, max_pages):
    requests, rows, lanes = mix.shape
    return pl.pallas_call(
        functools.partial(merge_kernel, max_pages=max_pages),
        out_shape=jax.ShapeDtypeStruct(mix.shape, jnp.bfloat16),
        in_specs=[SMEM_SPEC, VMEM_SPEC, VMEM_SPEC, VMEM_SPEC],
        out_specs=VMEM_SPEC,
        scratch_shapes=[pltpu.VMEM((2 * CAP * rows, lanes), jnp.float32)],
        compiler_params=pltpu.CompilerParams(vmem_limit_bytes=VMEM_LIMIT),
    )(slots, served, mix, stat)


def exchange(value):
    return lax.all_to_all(value, "group", split_axis=0, concat_axis=0, tiled=True)


def on_device(
    queries, fresh_kv, page_pool, context_len, page_holder, page_index, hot_owner, hot_pages
):
    requests, steps, local_heads, head_dim = queries.shape
    max_pages = page_holder.shape[1]
    groups = lax.axis_size("group")
    factor = math.log2(math.e) / math.sqrt(head_dim)
    q = queries.reshape(requests, steps * local_heads, head_dim)
    fresh = fresh_kv[:, :, 0].transpose(0, 2, 1, 3)
    pool = page_pool[:, 0]
    body = CAP * steps * local_heads
    dealt = exchange(deal(hot_pages, pool))
    asked, slots = ask(context_len, page_holder, page_index, q, groups, page_pool.shape[3])
    asked, dealt = lax.optimization_barrier((asked, dealt))
    share = lax.dynamic_index_in_dim(dealt, hot_owner[0], 0, keepdims=False)
    hot = lax.all_gather(share, "group", axis=0, tiled=False)

    def attend(sent, pages):
        sent = exchange(sent)
        table = sent[:, body : body + CAP, 0:2].astype(jnp.int32).reshape(-1)
        return serve(table, sent, pages, factor)

    def nothing(sent, pages):
        return jnp.zeros_like(sent)

    served = lax.cond(hot_owner[0] >= 0, attend, nothing, asked, pool)
    served = exchange(served)
    mix, stat = near(q, fresh, hot, factor, local_heads)
    attended = merge(slots, served, mix, stat, max_pages)
    return attended.reshape(requests, steps, local_heads, head_dim)


def solution(mesh):
    placed = (
        P("group", None, "head", None),
        P("group", None, "head", None, None),
        P("group", "head", None, None, None),
        P("group"),
        P("group", None),
        P("group", None),
        P(),
        P(),
    )
    return jax.shard_map(
        on_device,
        mesh=mesh,
        in_specs=placed,
        out_specs=P("group", None, "head", None),
        check_vma=False,
    )
```

```python
import functools
import math

import jax
import jax.numpy as jnp
from jax import lax
from jax.experimental import pallas as pl
from jax.experimental.pallas import tpu as pltpu
from jax.sharding import PartitionSpec as P

NEG_FILL = -1e30
CAP = 2
EXTRA = 8
MERGE_BLOCK = 2
VMEM_LIMIT = 48 * 1024 * 1024
HOT_VMEM_LIMIT = 56 * 1024 * 1024

SMEM_SPEC = pl.BlockSpec(memory_space=pltpu.SMEM)
HBM_SPEC = pl.BlockSpec(memory_space=pltpu.HBM)
VMEM_SPEC = pl.BlockSpec(memory_space=pltpu.VMEM)


def deal_kernel(hot_ref, pool_ref, out_ref, sems):
    copies = []
    for i in range(hot_ref.shape[0]):
        page = jnp.clip(hot_ref[i], 0, pool_ref.shape[0] - 1)
        copies.append(
            pltpu.make_async_copy(pool_ref.at[page], out_ref.at[pl.ds(2 * i, 2)], sems.at[i])
        )
    for copy in copies:
        copy.start()
    for copy in copies:
        copy.wait()


def deal(hot_pages, pool):
    _, two, page_len, head_dim = pool.shape
    return pl.pallas_call(
        deal_kernel,
        out_shape=jax.ShapeDtypeStruct((two * hot_pages.shape[0], page_len, head_dim), pool.dtype),
        in_specs=[SMEM_SPEC, HBM_SPEC],
        out_specs=VMEM_SPEC,
        scratch_shapes=[pltpu.SemaphoreType.DMA((hot_pages.shape[0],))],
        compiler_params=pltpu.CompilerParams(vmem_limit_bytes=VMEM_LIMIT),
    )(hot_pages, pool)


def ask_kernel(len_ref, holder_ref, index_ref, q_ref, ask_ref, slot_ref, count_ref, *, page_len):
    requests, max_pages = holder_ref.shape
    groups = ask_ref.shape[0]
    rows = q_ref.shape[1]
    body = CAP * rows
    lanes = ask_ref.shape[2]

    def clear(g, carry):
        count_ref[g] = 0
        ask_ref[g, pl.ds(body, EXTRA), :] = jnp.zeros((EXTRA, lanes), ask_ref.dtype)
        return carry

    lax.fori_loop(0, groups, clear, 0)
    sub = lax.broadcasted_iota(jnp.int32, (EXTRA, lanes), 0)
    lane = lax.broadcasted_iota(jnp.int32, (EXTRA, lanes), 1)

    def one(i, carry):
        r = i // max_pages
        p = i - r * max_pages
        filled = jnp.clip(len_ref[r] - p * page_len, 0, page_len)
        slot_ref[i] = -1

        @pl.when(filled > 0)
        def _():
            h = holder_ref[r, p]
            rank = jnp.minimum(count_ref[h], CAP - 1)
            count_ref[h] = rank + 1
            slot_ref[i] = h * CAP + rank
            ask_ref[h, pl.ds(pl.multiple_of(rank * rows, rows), rows), :] = q_ref[r]
            page = index_ref[r, p].astype(jnp.float32)
            old = ask_ref[h, pl.ds(body, EXTRA), :].astype(jnp.float32)
            new = jnp.where(lane == 0, page, filled.astype(jnp.float32))
            ask_ref[h, pl.ds(body, EXTRA), :] = jnp.where(
                (sub == rank) & (lane < 2), new, old
            ).astype(ask_ref.dtype)

        return carry

    lax.fori_loop(0, requests * max_pages, one, 0)


def ask(context_len, page_holder, page_index, q, groups, page_len):
    requests, max_pages = page_holder.shape
    rows, lanes = q.shape[1:]
    return pl.pallas_call(
        functools.partial(ask_kernel, page_len=page_len),
        out_shape=(
            jax.ShapeDtypeStruct((groups, CAP * rows + EXTRA, lanes), q.dtype),
            jax.ShapeDtypeStruct((requests * max_pages,), jnp.int32),
        ),
        in_specs=[SMEM_SPEC, SMEM_SPEC, SMEM_SPEC, VMEM_SPEC],
        out_specs=(VMEM_SPEC, SMEM_SPEC),
        scratch_shapes=[pltpu.SMEM((groups,), jnp.int32)],
        compiler_params=pltpu.CompilerParams(vmem_limit_bytes=VMEM_LIMIT),
    )(context_len, page_holder, page_index, q)


def serve_kernel(table_ref, asked_ref, pool_ref, out_ref, *, factor, block):
    groups, tall, lanes = asked_ref.shape
    body = tall - EXTRA
    rows = body // CAP
    page_len = pool_ref.shape[2]
    token = lax.broadcasted_iota(jnp.int32, (rows, page_len), 1)
    column = lax.broadcasted_iota(jnp.int32, (body, lanes), 1)
    sub = lax.broadcasted_iota(jnp.int32, (EXTRA, lanes), 0)

    def one(step, carry):
        scores = []
        pages = []
        for g in range(block):
            for s in range(CAP):
                at = ((step * block + g) * CAP + s) * 2
                page = jnp.clip(table_ref[at], 0, pool_ref.shape[0] - 1)
                sc = lax.dot_general(
                    asked_ref[step * block + g, s * rows : (s + 1) * rows, :],
                    pool_ref[page, 0],
                    (((1,), (1,)), ((), ())),
                    preferred_element_type=jnp.float32,
                )
                scores.append(jnp.where(token < table_ref[at + 1], sc * factor, NEG_FILL))
                pages.append(page)
        stats = jnp.zeros((body, lanes), jnp.float32)
        for g in range(block):
            both = []
            for s in range(CAP):
                sc = scores[g * CAP + s]
                top = jnp.max(sc, axis=1, keepdims=True)
                ex = jnp.exp2(sc - top)
                total = jnp.sum(ex, axis=1, keepdims=True)
                mix = jnp.dot(
                    ex.astype(jnp.bfloat16),
                    pool_ref[pages[g * CAP + s], 1],
                    preferred_element_type=jnp.float32,
                )
                out_ref[step * block + g, s * rows : (s + 1) * rows, :] = (
                    mix * (1.0 / total)
                ).astype(out_ref.dtype)
                both.append(top + jnp.log2(total))
            stats = jnp.where(column == g, jnp.concatenate(both, axis=0), stats)
        flat = stats.T
        high = flat.astype(jnp.bfloat16).astype(jnp.float32)
        low = flat - high
        for g in range(block):
            tile = jnp.where(sub == 0, high[g : g + 1], jnp.where(sub == 1, low[g : g + 1], 0.0))
            out_ref[step * block + g, body : body + EXTRA, :] = tile.astype(out_ref.dtype)
        return carry

    lax.fori_loop(0, groups // block, one, 0)


def serve(table, asked, pool, factor):
    block = math.gcd(asked.shape[0], 16)
    return pl.pallas_call(
        functools.partial(serve_kernel, factor=factor, block=block),
        out_shape=jax.ShapeDtypeStruct(asked.shape, asked.dtype),
        in_specs=[SMEM_SPEC, VMEM_SPEC, VMEM_SPEC],
        out_specs=VMEM_SPEC,
        compiler_params=pltpu.CompilerParams(vmem_limit_bytes=VMEM_LIMIT),
    )(table, asked, pool)


def merge_kernel(
    slot_ref, q_ref, fresh_ref, served_ref, mix_ref, stat_ref, lse_ref, *, factor, per_kv, max_pages
):
    groups = served_ref.shape[0]
    requests, rows, lanes = mix_ref.shape
    steps = fresh_ref.shape[2]
    block = math.gcd(requests, MERGE_BLOCK)
    body = CAP * rows

    def unpack(g, carry):
        tile = served_ref[g, pl.ds(body, EXTRA), :].astype(jnp.float32)
        lse_ref[pl.ds(g, 1), :] = tile[0:1] + tile[1:2]
        return carry

    lax.fori_loop(0, groups, unpack, 0)
    lse_ref[pl.ds(body, body), :] = lse_ref[pl.ds(0, body), :].T
    column = lax.broadcasted_iota(jnp.int32, (rows, lanes), 1)
    row_step = lax.broadcasted_iota(jnp.int32, (rows, steps), 0) // per_kv
    key_step = lax.broadcasted_iota(jnp.int32, (rows, steps), 1)

    def one(n, carry):
        for b in range(block):
            merge_one(n * block + b)
        return carry

    def merge_one(r):
        sc = lax.dot_general(
            q_ref[r],
            fresh_ref[r, 0],
            (((1,), (1,)), ((), ())),
            preferred_element_type=jnp.float32,
        )
        sc = jnp.where(key_step <= row_step, sc * factor, NEG_FILL)
        own_top = jnp.max(sc, axis=1, keepdims=True)
        ex = jnp.exp2(sc - own_top)
        own_total = jnp.sum(ex, axis=1, keepdims=True)
        own = jnp.dot(
            ex.astype(jnp.bfloat16), fresh_ref[r, 1], preferred_element_type=jnp.float32
        )
        places = []
        tops = []
        top = own_top
        for p in range(max_pages):
            slot = slot_ref[r * max_pages + p]
            safe = jnp.maximum(slot, 0)
            h = safe // CAP
            start = pl.multiple_of((safe - h * CAP) * rows, rows)
            picked = lse_ref[pl.ds(body + start, rows), :]
            lse = jnp.sum(jnp.where(column == h, picked, 0.0), axis=1, keepdims=True)
            lse = jnp.where(slot >= 0, lse, NEG_FILL)
            places.append((slot, h, start))
            tops.append(lse)
            top = jnp.maximum(top, lse)
        weight = jnp.exp2(own_top - top)
        total = own_total * weight
        mix = own * weight
        for (slot, h, start), lse in zip(places, tops):
            weight = jnp.exp2(lse - top)
            total = total + weight
            part = served_ref[h, pl.ds(start, rows), :]
            mix = mix + jnp.where(slot >= 0, part.astype(jnp.float32) * weight, 0.0)
        mix_ref[r] = mix
        stat_ref[r] = jnp.where(column == 0, top, total)

    lax.fori_loop(0, requests // block, one, 0)


def merge(slots, q, fresh, served, factor, per_kv, max_pages):
    requests, rows, lanes = q.shape
    return pl.pallas_call(
        functools.partial(merge_kernel, factor=factor, per_kv=per_kv, max_pages=max_pages),
        out_shape=(
            jax.ShapeDtypeStruct(q.shape, jnp.float32),
            jax.ShapeDtypeStruct(q.shape, jnp.float32),
        ),
        in_specs=[SMEM_SPEC] + [VMEM_SPEC] * 3,
        out_specs=(VMEM_SPEC, VMEM_SPEC),
        scratch_shapes=[pltpu.VMEM((2 * CAP * rows, lanes), jnp.float32)],
        compiler_params=pltpu.CompilerParams(vmem_limit_bytes=VMEM_LIMIT),
    )(slots, q, fresh, served)


def hot_kernel(q_ref, mix_ref, stat_ref, hot_ref, out_ref, kv_ref, sems, *, factor, block):
    chunks, per_chunk, _, page_len, lanes = hot_ref.shape
    copies = [
        [
            pltpu.make_async_copy(hot_ref.at[c, :, part], kv_ref.at[c, part], sems.at[c, part])
            for part in range(2)
        ]
        for c in range(chunks)
    ]
    for pair in copies:
        for copy in pair:
            copy.start()
    requests, rows, _ = q_ref.shape
    for n in range(requests // block):
        at = slice(n * block, (n + 1) * block)
        q = q_ref[at].reshape(block * rows, lanes)
        stat = stat_ref[at].reshape(block * rows, lanes)
        top = stat[:, 0:1]
        total = stat[:, 1:2]
        mix = mix_ref[at].reshape(block * rows, lanes)
        for c in range(chunks):
            if n == 0:
                for copy in copies[c]:
                    copy.wait()
            sc = lax.dot_general(
                q,
                kv_ref[c, 0].reshape(per_chunk * page_len, lanes),
                (((1,), (1,)), ((), ())),
                preferred_element_type=jnp.float32,
            )
            new_top = jnp.maximum(top, jnp.max(sc, axis=1, keepdims=True) * factor)
            ex = jnp.exp2(sc * factor - new_top)
            keep = jnp.exp2(top - new_top)
            total = total * keep + jnp.sum(ex, axis=1, keepdims=True)
            mix = mix * keep + jnp.dot(
                ex.astype(jnp.bfloat16),
                kv_ref[c, 1].reshape(per_chunk * page_len, lanes),
                preferred_element_type=jnp.float32,
            )
            top = new_top
        out_ref[at] = (mix / total).astype(out_ref.dtype).reshape(block, rows, lanes)


def attend_hot(q, mix, stat, hot, factor):
    requests, rows, lanes = q.shape
    pages = hot.shape[0] // 2
    page_len = hot.shape[1]
    block = math.gcd(requests, 8)
    chunks = math.gcd(pages, 8)
    hot = hot.reshape(chunks, pages // chunks, 2, page_len, lanes)
    return pl.pallas_call(
        functools.partial(hot_kernel, factor=factor, block=block),
        out_shape=jax.ShapeDtypeStruct(q.shape, q.dtype),
        in_specs=[VMEM_SPEC] * 3 + [HBM_SPEC],
        out_specs=VMEM_SPEC,
        scratch_shapes=[
            pltpu.VMEM((chunks, 2, pages // chunks, page_len, lanes), hot.dtype),
            pltpu.SemaphoreType.DMA((chunks, 2)),
        ],
        compiler_params=pltpu.CompilerParams(vmem_limit_bytes=HOT_VMEM_LIMIT),
    )(q, mix, stat, hot)


def exchange(value):
    return lax.all_to_all(value, "group", split_axis=0, concat_axis=0, tiled=True)


def on_device(
    queries, fresh_kv, page_pool, context_len, page_holder, page_index, hot_owner, hot_pages
):
    requests, steps, local_heads, head_dim = queries.shape
    max_pages = page_holder.shape[1]
    groups = lax.axis_size("group")
    factor = math.log2(math.e) / math.sqrt(head_dim)
    q = queries.reshape(requests, steps * local_heads, head_dim)
    fresh = fresh_kv[:, :, 0].transpose(0, 2, 1, 3)
    pool = page_pool[:, 0]
    body = CAP * steps * local_heads
    dealt = exchange(deal(hot_pages, pool))
    asked, slots = ask(context_len, page_holder, page_index, q, groups, page_pool.shape[3])
    asked, dealt = lax.optimization_barrier((asked, dealt))
    share = lax.dynamic_index_in_dim(dealt, hot_owner[0], 0, keepdims=False)
    hot = lax.all_gather(share, "group", axis=0, tiled=False)

    def attend(sent, pages):
        sent = exchange(sent)
        table = sent[:, body : body + CAP, 0:2].astype(jnp.int32).reshape(-1)
        return serve(table, sent, pages, factor)

    def nothing(sent, pages):
        return jnp.zeros_like(sent)

    served = lax.cond(hot_owner[0] >= 0, attend, nothing, asked, pool)
    served = exchange(served)
    mix, stat = merge(slots, q, fresh, served, factor, local_heads, max_pages)
    attended = attend_hot(q, mix, stat, hot, factor)
    return attended.reshape(requests, steps, local_heads, head_dim)


def solution(mesh):
    placed = (
        P("group", None, "head", None),
        P("group", None, "head", None, None),
        P("group", "head", None, None, None),
        P("group"),
        P("group", None),
        P("group", None),
        P(),
        P(),
    )
    return jax.shard_map(
        on_device,
        mesh=mesh,
        in_specs=placed,
        out_specs=P("group", None, "head", None),
        check_vma=False,
    )
```

```python
import functools
import math

import jax
import jax.numpy as jnp
from jax import lax
from jax.experimental import pallas as pl
from jax.experimental.pallas import tpu as pltpu
from jax.sharding import PartitionSpec as P

NEG_FILL = -1e30
CAP = 2
EXTRA = 8
MERGE_BLOCK = 2
VMEM_LIMIT = 48 * 1024 * 1024

SMEM_SPEC = pl.BlockSpec(memory_space=pltpu.SMEM)
HBM_SPEC = pl.BlockSpec(memory_space=pltpu.HBM)
VMEM_SPEC = pl.BlockSpec(memory_space=pltpu.VMEM)


def deal_kernel(hot_ref, pool_ref, out_ref, sems):
    copies = []
    for i in range(hot_ref.shape[0]):
        page = jnp.clip(hot_ref[i], 0, pool_ref.shape[0] - 1)
        copies.append(
            pltpu.make_async_copy(pool_ref.at[page], out_ref.at[pl.ds(2 * i, 2)], sems.at[i])
        )
    for copy in copies:
        copy.start()
    for copy in copies:
        copy.wait()


def deal(hot_pages, pool):
    _, two, page_len, head_dim = pool.shape
    return pl.pallas_call(
        deal_kernel,
        out_shape=jax.ShapeDtypeStruct((two * hot_pages.shape[0], page_len, head_dim), pool.dtype),
        in_specs=[SMEM_SPEC, HBM_SPEC],
        out_specs=VMEM_SPEC,
        scratch_shapes=[pltpu.SemaphoreType.DMA((hot_pages.shape[0],))],
        compiler_params=pltpu.CompilerParams(vmem_limit_bytes=VMEM_LIMIT),
    )(hot_pages, pool)


def ask_kernel(len_ref, holder_ref, index_ref, q_ref, ask_ref, slot_ref, count_ref, *, page_len):
    requests, max_pages = holder_ref.shape
    groups = ask_ref.shape[0]
    rows = q_ref.shape[1]
    body = CAP * rows
    lanes = ask_ref.shape[2]

    def clear(g, carry):
        count_ref[g] = 0
        ask_ref[g, pl.ds(body, EXTRA), :] = jnp.zeros((EXTRA, lanes), ask_ref.dtype)
        return carry

    lax.fori_loop(0, groups, clear, 0)
    sub = lax.broadcasted_iota(jnp.int32, (EXTRA, lanes), 0)
    lane = lax.broadcasted_iota(jnp.int32, (EXTRA, lanes), 1)

    def one(i, carry):
        r = i // max_pages
        p = i - r * max_pages
        filled = jnp.clip(len_ref[r] - p * page_len, 0, page_len)
        slot_ref[i] = -1

        @pl.when(filled > 0)
        def _():
            h = holder_ref[r, p]
            rank = jnp.minimum(count_ref[h], CAP - 1)
            count_ref[h] = rank + 1
            slot_ref[i] = h * CAP + rank
            ask_ref[h, pl.ds(pl.multiple_of(rank * rows, rows), rows), :] = q_ref[r]
            page = index_ref[r, p].astype(jnp.float32)
            old = ask_ref[h, pl.ds(body, EXTRA), :].astype(jnp.float32)
            new = jnp.where(lane == 0, page, filled.astype(jnp.float32))
            ask_ref[h, pl.ds(body, EXTRA), :] = jnp.where(
                (sub == rank) & (lane < 2), new, old
            ).astype(ask_ref.dtype)

        return carry

    lax.fori_loop(0, requests * max_pages, one, 0)


def ask(context_len, page_holder, page_index, q, groups, page_len):
    requests, max_pages = page_holder.shape
    rows, lanes = q.shape[1:]
    return pl.pallas_call(
        functools.partial(ask_kernel, page_len=page_len),
        out_shape=(
            jax.ShapeDtypeStruct((groups, CAP * rows + EXTRA, lanes), q.dtype),
            jax.ShapeDtypeStruct((requests * max_pages,), jnp.int32),
        ),
        in_specs=[SMEM_SPEC, SMEM_SPEC, SMEM_SPEC, VMEM_SPEC],
        out_specs=(VMEM_SPEC, SMEM_SPEC),
        scratch_shapes=[pltpu.SMEM((groups,), jnp.int32)],
        compiler_params=pltpu.CompilerParams(vmem_limit_bytes=VMEM_LIMIT),
    )(context_len, page_holder, page_index, q)


def serve_kernel(table_ref, asked_ref, pool_ref, out_ref, *, factor, block):
    groups, tall, lanes = asked_ref.shape
    body = tall - EXTRA
    rows = body // CAP
    page_len = pool_ref.shape[2]
    token = lax.broadcasted_iota(jnp.int32, (rows, page_len), 1)
    column = lax.broadcasted_iota(jnp.int32, (body, lanes), 1)
    sub = lax.broadcasted_iota(jnp.int32, (EXTRA, lanes), 0)

    def one(step, carry):
        scores = []
        pages = []
        for g in range(block):
            for s in range(CAP):
                at = ((step * block + g) * CAP + s) * 2
                page = jnp.clip(table_ref[at], 0, pool_ref.shape[0] - 1)
                sc = lax.dot_general(
                    asked_ref[step * block + g, s * rows : (s + 1) * rows, :],
                    pool_ref[page, 0],
                    (((1,), (1,)), ((), ())),
                    preferred_element_type=jnp.float32,
                )
                scores.append(jnp.where(token < table_ref[at + 1], sc * factor, NEG_FILL))
                pages.append(page)
        stats = jnp.zeros((body, lanes), jnp.float32)
        for g in range(block):
            both = []
            for s in range(CAP):
                sc = scores[g * CAP + s]
                top = jnp.max(sc, axis=1, keepdims=True)
                ex = jnp.exp2(sc - top)
                total = jnp.sum(ex, axis=1, keepdims=True)
                mix = jnp.dot(
                    ex.astype(jnp.bfloat16),
                    pool_ref[pages[g * CAP + s], 1],
                    preferred_element_type=jnp.float32,
                )
                out_ref[step * block + g, s * rows : (s + 1) * rows, :] = (
                    mix * (1.0 / total)
                ).astype(out_ref.dtype)
                both.append(top + jnp.log2(total))
            stats = jnp.where(column == g, jnp.concatenate(both, axis=0), stats)
        flat = stats.T
        high = flat.astype(jnp.bfloat16).astype(jnp.float32)
        low = flat - high
        for g in range(block):
            tile = jnp.where(sub == 0, high[g : g + 1], jnp.where(sub == 1, low[g : g + 1], 0.0))
            out_ref[step * block + g, body : body + EXTRA, :] = tile.astype(out_ref.dtype)
        return carry

    lax.fori_loop(0, groups // block, one, 0)


def serve(table, asked, pool, factor):
    block = math.gcd(asked.shape[0], 16)
    return pl.pallas_call(
        functools.partial(serve_kernel, factor=factor, block=block),
        out_shape=jax.ShapeDtypeStruct(asked.shape, asked.dtype),
        in_specs=[SMEM_SPEC, VMEM_SPEC, VMEM_SPEC],
        out_specs=VMEM_SPEC,
        compiler_params=pltpu.CompilerParams(vmem_limit_bytes=VMEM_LIMIT),
    )(table, asked, pool)


def merge_kernel(
    slot_ref, q_ref, fresh_ref, served_ref, mix_ref, stat_ref, lse_ref, *, factor, per_kv, max_pages
):
    groups = served_ref.shape[0]
    requests, rows, lanes = mix_ref.shape
    steps = fresh_ref.shape[2]
    block = math.gcd(requests, MERGE_BLOCK)
    body = CAP * rows

    def unpack(g, carry):
        tile = served_ref[g, pl.ds(body, EXTRA), :].astype(jnp.float32)
        lse_ref[pl.ds(g, 1), :] = tile[0:1] + tile[1:2]
        return carry

    lax.fori_loop(0, groups, unpack, 0)
    lse_ref[pl.ds(body, body), :] = lse_ref[pl.ds(0, body), :].T
    column = lax.broadcasted_iota(jnp.int32, (rows, lanes), 1)
    row_step = lax.broadcasted_iota(jnp.int32, (rows, steps), 0) // per_kv
    key_step = lax.broadcasted_iota(jnp.int32, (rows, steps), 1)

    def one(n, carry):
        for b in range(block):
            merge_one(n * block + b)
        return carry

    def merge_one(r):
        sc = lax.dot_general(
            q_ref[r],
            fresh_ref[r, 0],
            (((1,), (1,)), ((), ())),
            preferred_element_type=jnp.float32,
        )
        sc = jnp.where(key_step <= row_step, sc * factor, NEG_FILL)
        own_top = jnp.max(sc, axis=1, keepdims=True)
        ex = jnp.exp2(sc - own_top)
        own_total = jnp.sum(ex, axis=1, keepdims=True)
        own = jnp.dot(
            ex.astype(jnp.bfloat16), fresh_ref[r, 1], preferred_element_type=jnp.float32
        )
        places = []
        tops = []
        top = own_top
        for p in range(max_pages):
            slot = slot_ref[r * max_pages + p]
            safe = jnp.maximum(slot, 0)
            h = safe // CAP
            start = pl.multiple_of((safe - h * CAP) * rows, rows)
            picked = lse_ref[pl.ds(body + start, rows), :]
            lse = jnp.sum(jnp.where(column == h, picked, 0.0), axis=1, keepdims=True)
            lse = jnp.where(slot >= 0, lse, NEG_FILL)
            places.append((slot, h, start))
            tops.append(lse)
            top = jnp.maximum(top, lse)
        weight = jnp.exp2(own_top - top)
        total = own_total * weight
        mix = own * weight
        for (slot, h, start), lse in zip(places, tops):
            weight = jnp.exp2(lse - top)
            total = total + weight
            part = served_ref[h, pl.ds(start, rows), :]
            mix = mix + jnp.where(slot >= 0, part.astype(jnp.float32) * weight, 0.0)
        mix_ref[r] = mix
        stat_ref[r] = jnp.where(column == 0, top, total)

    lax.fori_loop(0, requests // block, one, 0)


def merge(slots, q, fresh, served, factor, per_kv, max_pages):
    requests, rows, lanes = q.shape
    return pl.pallas_call(
        functools.partial(merge_kernel, factor=factor, per_kv=per_kv, max_pages=max_pages),
        out_shape=(
            jax.ShapeDtypeStruct(q.shape, jnp.float32),
            jax.ShapeDtypeStruct(q.shape, jnp.float32),
        ),
        in_specs=[SMEM_SPEC] + [VMEM_SPEC] * 3,
        out_specs=(VMEM_SPEC, VMEM_SPEC),
        scratch_shapes=[pltpu.VMEM((2 * CAP * rows, lanes), jnp.float32)],
        compiler_params=pltpu.CompilerParams(vmem_limit_bytes=VMEM_LIMIT),
    )(slots, q, fresh, served)


def hot_kernel(q_ref, mix_ref, stat_ref, hot_ref, out_ref, *, factor, block):
    chunks, per_chunk, _, page_len, lanes = hot_ref.shape
    requests, rows, _ = q_ref.shape

    def one(n, carry):
        at = pl.ds(n * block, block)
        q = q_ref[at].reshape(block * rows, lanes)
        stat = stat_ref[at].reshape(block * rows, lanes)
        lane = lax.broadcasted_iota(jnp.int32, stat.shape, 1)
        top = jnp.max(jnp.where(lane == 0, stat, 2 * NEG_FILL), axis=1, keepdims=True)
        total = jnp.sum(jnp.where(lane == 1, stat, 0.0), axis=1, keepdims=True)
        mix = mix_ref[at].reshape(block * rows, lanes)
        for c in range(chunks):
            sc = lax.dot_general(
                q,
                hot_ref[c, :, 0].reshape(per_chunk * page_len, lanes),
                (((1,), (1,)), ((), ())),
                preferred_element_type=jnp.float32,
            )
            new_top = jnp.maximum(top, jnp.max(sc, axis=1, keepdims=True) * factor)
            ex = jnp.exp2(sc * factor - new_top)
            keep = jnp.exp2(top - new_top)
            total = total * keep + jnp.sum(ex, axis=1, keepdims=True)
            mix = mix * keep + jnp.dot(
                ex.astype(jnp.bfloat16),
                hot_ref[c, :, 1].reshape(per_chunk * page_len, lanes),
                preferred_element_type=jnp.float32,
            )
            top = new_top
        out_ref[at] = (mix / total).astype(out_ref.dtype).reshape(block, rows, lanes)
        return carry

    lax.fori_loop(0, requests // block, one, 0)


def attend_hot(q, mix, stat, hot, factor):
    requests, rows, lanes = q.shape
    pages = hot.shape[0] // 2
    page_len = hot.shape[1]
    block = math.gcd(requests, 8)
    chunks = math.gcd(pages, 8)
    hot = hot.reshape(chunks, pages // chunks, 2, page_len, lanes)
    return pl.pallas_call(
        functools.partial(hot_kernel, factor=factor, block=block),
        out_shape=jax.ShapeDtypeStruct(q.shape, q.dtype),
        in_specs=[VMEM_SPEC] * 4,
        out_specs=VMEM_SPEC,
        compiler_params=pltpu.CompilerParams(vmem_limit_bytes=VMEM_LIMIT),
    )(q, mix, stat, hot)


def exchange(value):
    return lax.all_to_all(value, "group", split_axis=0, concat_axis=0, tiled=True)


def on_device(
    queries, fresh_kv, page_pool, context_len, page_holder, page_index, hot_owner, hot_pages
):
    requests, steps, local_heads, head_dim = queries.shape
    max_pages = page_holder.shape[1]
    groups = lax.axis_size("group")
    factor = math.log2(math.e) / math.sqrt(head_dim)
    q = queries.reshape(requests, steps * local_heads, head_dim)
    fresh = fresh_kv[:, :, 0].transpose(0, 2, 1, 3)
    pool = page_pool[:, 0]
    body = CAP * steps * local_heads
    dealt = exchange(deal(hot_pages, pool))
    asked, slots = ask(context_len, page_holder, page_index, q, groups, page_pool.shape[3])
    asked, dealt = lax.optimization_barrier((asked, dealt))
    share = lax.dynamic_index_in_dim(dealt, hot_owner[0], 0, keepdims=False)
    asked, share = lax.optimization_barrier((asked, share))
    hot = lax.all_gather(share, "group", axis=0, tiled=False)

    def attend(sent, pages, slots, q, fresh):
        sent = exchange(sent)
        table = sent[:, body : body + CAP, 0:2].astype(jnp.int32).reshape(-1)
        served = exchange(serve(table, sent, pages, factor))
        return merge(slots, q, fresh, served, factor, local_heads, max_pages)

    def nothing(sent, pages, slots, q, fresh):
        return (jnp.zeros(q.shape, jnp.float32),) * 2

    mix, stat = lax.cond(hot_owner[0] >= 0, attend, nothing, asked, pool, slots, q, fresh)
    attended = attend_hot(q, mix, stat, hot, factor)
    return attended.reshape(requests, steps, local_heads, head_dim)


def solution(mesh):
    placed = (
        P("group", None, "head", None),
        P("group", None, "head", None, None),
        P("group", "head", None, None, None),
        P("group"),
        P("group", None),
        P("group", None),
        P(),
        P(),
    )
    return jax.shard_map(
        on_device,
        mesh=mesh,
        in_specs=placed,
        out_specs=P("group", None, "head", None),
        check_vma=False,
    )
```

```python
import functools
import math

import jax
import jax.numpy as jnp
from jax import lax
from jax.experimental import pallas as pl
from jax.experimental.pallas import tpu as pltpu
from jax.sharding import PartitionSpec as P

NEG_FILL = -1e30
CAP = 2
EXTRA = 8
MERGE_BLOCK = 2
VMEM_LIMIT = 48 * 1024 * 1024

SMEM_SPEC = pl.BlockSpec(memory_space=pltpu.SMEM)
HBM_SPEC = pl.BlockSpec(memory_space=pltpu.HBM)
VMEM_SPEC = pl.BlockSpec(memory_space=pltpu.VMEM)


def deal_kernel(hot_ref, pool_ref, out_ref, sems):
    copies = []
    for i in range(hot_ref.shape[0]):
        page = jnp.clip(hot_ref[i], 0, pool_ref.shape[0] - 1)
        copies.append(
            pltpu.make_async_copy(pool_ref.at[page], out_ref.at[pl.ds(2 * i, 2)], sems.at[i])
        )
    for copy in copies:
        copy.start()
    for copy in copies:
        copy.wait()


def deal(hot_pages, pool):
    _, two, page_len, head_dim = pool.shape
    return pl.pallas_call(
        deal_kernel,
        out_shape=jax.ShapeDtypeStruct((two * hot_pages.shape[0], page_len, head_dim), pool.dtype),
        in_specs=[SMEM_SPEC, HBM_SPEC],
        out_specs=VMEM_SPEC,
        scratch_shapes=[pltpu.SemaphoreType.DMA((hot_pages.shape[0],))],
        compiler_params=pltpu.CompilerParams(vmem_limit_bytes=VMEM_LIMIT),
    )(hot_pages, pool)


def ask_kernel(len_ref, holder_ref, index_ref, q_ref, ask_ref, slot_ref, count_ref, *, page_len):
    requests, max_pages = holder_ref.shape
    groups = ask_ref.shape[0]
    rows = q_ref.shape[1]
    body = CAP * rows
    lanes = ask_ref.shape[2]

    def clear(g, carry):
        count_ref[g] = 0
        ask_ref[g, pl.ds(body, EXTRA), :] = jnp.zeros((EXTRA, lanes), ask_ref.dtype)
        return carry

    lax.fori_loop(0, groups, clear, 0)
    sub = lax.broadcasted_iota(jnp.int32, (EXTRA, lanes), 0)
    lane = lax.broadcasted_iota(jnp.int32, (EXTRA, lanes), 1)

    def one(i, carry):
        r = i // max_pages
        p = i - r * max_pages
        filled = jnp.clip(len_ref[r] - p * page_len, 0, page_len)
        slot_ref[i] = -1

        @pl.when(filled > 0)
        def _():
            h = holder_ref[r, p]
            rank = jnp.minimum(count_ref[h], CAP - 1)
            count_ref[h] = rank + 1
            slot_ref[i] = h * CAP + rank
            ask_ref[h, pl.ds(pl.multiple_of(rank * rows, rows), rows), :] = q_ref[r]
            page = index_ref[r, p].astype(jnp.float32)
            old = ask_ref[h, pl.ds(body, EXTRA), :].astype(jnp.float32)
            new = jnp.where(lane == 0, page, filled.astype(jnp.float32))
            ask_ref[h, pl.ds(body, EXTRA), :] = jnp.where(
                (sub == rank) & (lane < 2), new, old
            ).astype(ask_ref.dtype)

        return carry

    lax.fori_loop(0, requests * max_pages, one, 0)


def ask(context_len, page_holder, page_index, q, groups, page_len):
    requests, max_pages = page_holder.shape
    rows, lanes = q.shape[1:]
    return pl.pallas_call(
        functools.partial(ask_kernel, page_len=page_len),
        out_shape=(
            jax.ShapeDtypeStruct((groups, CAP * rows + EXTRA, lanes), q.dtype),
            jax.ShapeDtypeStruct((requests * max_pages,), jnp.int32),
        ),
        in_specs=[SMEM_SPEC, SMEM_SPEC, SMEM_SPEC, VMEM_SPEC],
        out_specs=(VMEM_SPEC, SMEM_SPEC),
        scratch_shapes=[pltpu.SMEM((groups,), jnp.int32)],
        compiler_params=pltpu.CompilerParams(vmem_limit_bytes=VMEM_LIMIT),
    )(context_len, page_holder, page_index, q)


def serve_kernel(table_ref, asked_ref, pool_ref, out_ref, *, factor, block):
    groups, tall, lanes = asked_ref.shape
    body = tall - EXTRA
    rows = body // CAP
    page_len = pool_ref.shape[2]
    token = lax.broadcasted_iota(jnp.int32, (rows, page_len), 1)
    column = lax.broadcasted_iota(jnp.int32, (body, lanes), 1)
    sub = lax.broadcasted_iota(jnp.int32, (EXTRA, lanes), 0)

    def one(step, carry):
        scores = []
        pages = []
        for g in range(block):
            for s in range(CAP):
                at = ((step * block + g) * CAP + s) * 2
                page = jnp.clip(table_ref[at], 0, pool_ref.shape[0] - 1)
                sc = lax.dot_general(
                    asked_ref[step * block + g, s * rows : (s + 1) * rows, :],
                    pool_ref[page, 0],
                    (((1,), (1,)), ((), ())),
                    preferred_element_type=jnp.float32,
                )
                scores.append(jnp.where(token < table_ref[at + 1], sc * factor, NEG_FILL))
                pages.append(page)
        stats = jnp.zeros((body, lanes), jnp.float32)
        for g in range(block):
            both = []
            for s in range(CAP):
                sc = scores[g * CAP + s]
                top = jnp.max(sc, axis=1, keepdims=True)
                ex = jnp.exp2(sc - top)
                total = jnp.sum(ex, axis=1, keepdims=True)
                mix = jnp.dot(
                    ex.astype(jnp.bfloat16),
                    pool_ref[pages[g * CAP + s], 1],
                    preferred_element_type=jnp.float32,
                )
                out_ref[step * block + g, s * rows : (s + 1) * rows, :] = (
                    mix * (1.0 / total)
                ).astype(out_ref.dtype)
                both.append(top + jnp.log2(total))
            stats = jnp.where(column == g, jnp.concatenate(both, axis=0), stats)
        flat = stats.T
        high = flat.astype(jnp.bfloat16).astype(jnp.float32)
        low = flat - high
        for g in range(block):
            tile = jnp.where(sub == 0, high[g : g + 1], jnp.where(sub == 1, low[g : g + 1], 0.0))
            out_ref[step * block + g, body : body + EXTRA, :] = tile.astype(out_ref.dtype)
        return carry

    lax.fori_loop(0, groups // block, one, 0)


def serve(table, asked, pool, factor):
    block = math.gcd(asked.shape[0], 16)
    return pl.pallas_call(
        functools.partial(serve_kernel, factor=factor, block=block),
        out_shape=jax.ShapeDtypeStruct(asked.shape, asked.dtype),
        in_specs=[SMEM_SPEC, VMEM_SPEC, VMEM_SPEC],
        out_specs=VMEM_SPEC,
        compiler_params=pltpu.CompilerParams(vmem_limit_bytes=VMEM_LIMIT),
    )(table, asked, pool)


def merge_kernel(
    slot_ref, q_ref, fresh_ref, served_ref, mix_ref, stat_ref, lse_ref, *, factor, per_kv, max_pages
):
    groups = served_ref.shape[0]
    requests, rows, lanes = mix_ref.shape
    steps = fresh_ref.shape[2]
    block = math.gcd(requests, MERGE_BLOCK)
    body = CAP * rows

    def unpack(g, carry):
        tile = served_ref[g, pl.ds(body, EXTRA), :].astype(jnp.float32)
        lse_ref[pl.ds(g, 1), :] = tile[0:1] + tile[1:2]
        return carry

    lax.fori_loop(0, groups, unpack, 0)
    lse_ref[pl.ds(body, body), :] = lse_ref[pl.ds(0, body), :].T
    column = lax.broadcasted_iota(jnp.int32, (rows, lanes), 1)
    row_step = lax.broadcasted_iota(jnp.int32, (rows, steps), 0) // per_kv
    key_step = lax.broadcasted_iota(jnp.int32, (rows, steps), 1)

    def one(n, carry):
        for b in range(block):
            merge_one(n * block + b)
        return carry

    def merge_one(r):
        sc = lax.dot_general(
            q_ref[r],
            fresh_ref[r, 0],
            (((1,), (1,)), ((), ())),
            preferred_element_type=jnp.float32,
        )
        sc = jnp.where(key_step <= row_step, sc * factor, NEG_FILL)
        own_top = jnp.max(sc, axis=1, keepdims=True)
        ex = jnp.exp2(sc - own_top)
        own_total = jnp.sum(ex, axis=1, keepdims=True)
        own = jnp.dot(
            ex.astype(jnp.bfloat16), fresh_ref[r, 1], preferred_element_type=jnp.float32
        )
        places = []
        tops = []
        top = own_top
        for p in range(max_pages):
            slot = slot_ref[r * max_pages + p]
            safe = jnp.maximum(slot, 0)
            h = safe // CAP
            start = pl.multiple_of((safe - h * CAP) * rows, rows)
            picked = lse_ref[pl.ds(body + start, rows), :]
            lse = jnp.sum(jnp.where(column == h, picked, 0.0), axis=1, keepdims=True)
            lse = jnp.where(slot >= 0, lse, NEG_FILL)
            places.append((slot, h, start))
            tops.append(lse)
            top = jnp.maximum(top, lse)
        weight = jnp.exp2(own_top - top)
        total = own_total * weight
        mix = own * weight
        for (slot, h, start), lse in zip(places, tops):
            weight = jnp.exp2(lse - top)
            total = total + weight
            part = served_ref[h, pl.ds(start, rows), :]
            mix = mix + jnp.where(slot >= 0, part.astype(jnp.float32) * weight, 0.0)
        mix_ref[r] = mix
        stat_ref[r] = jnp.where(column == 0, top, total)

    lax.fori_loop(0, requests // block, one, 0)


def merge(slots, q, fresh, served, factor, per_kv, max_pages):
    requests, rows, lanes = q.shape
    return pl.pallas_call(
        functools.partial(merge_kernel, factor=factor, per_kv=per_kv, max_pages=max_pages),
        out_shape=(
            jax.ShapeDtypeStruct(q.shape, jnp.float32),
            jax.ShapeDtypeStruct(q.shape, jnp.float32),
        ),
        in_specs=[SMEM_SPEC] + [VMEM_SPEC] * 3,
        out_specs=(VMEM_SPEC, VMEM_SPEC),
        scratch_shapes=[pltpu.VMEM((2 * CAP * rows, lanes), jnp.float32)],
        compiler_params=pltpu.CompilerParams(vmem_limit_bytes=VMEM_LIMIT),
    )(slots, q, fresh, served)


def hot_kernel(q_ref, mix_ref, stat_ref, hot_ref, out_ref, *, factor, block):
    chunks, per_chunk, _, page_len, lanes = hot_ref.shape
    requests, rows, _ = q_ref.shape

    def one(n, carry):
        at = pl.ds(n * block, block)
        q = q_ref[at].reshape(block * rows, lanes)
        stat = stat_ref[at].reshape(block * rows, lanes)
        lane = lax.broadcasted_iota(jnp.int32, stat.shape, 1)
        top = jnp.max(jnp.where(lane == 0, stat, 2 * NEG_FILL), axis=1, keepdims=True)
        total = jnp.sum(jnp.where(lane == 1, stat, 0.0), axis=1, keepdims=True)
        mix = mix_ref[at].reshape(block * rows, lanes)
        for c in range(chunks):
            sc = lax.dot_general(
                q,
                hot_ref[c, :, 0].reshape(per_chunk * page_len, lanes),
                (((1,), (1,)), ((), ())),
                preferred_element_type=jnp.float32,
            )
            new_top = jnp.maximum(top, jnp.max(sc, axis=1, keepdims=True) * factor)
            ex = jnp.exp2(sc * factor - new_top)
            keep = jnp.exp2(top - new_top)
            total = total * keep + jnp.sum(ex, axis=1, keepdims=True)
            mix = mix * keep + jnp.dot(
                ex.astype(jnp.bfloat16),
                hot_ref[c, :, 1].reshape(per_chunk * page_len, lanes),
                preferred_element_type=jnp.float32,
            )
            top = new_top
        out_ref[at] = (mix / total).astype(out_ref.dtype).reshape(block, rows, lanes)
        return carry

    lax.fori_loop(0, requests // block, one, 0)


def attend_hot(q, mix, stat, hot, factor):
    requests, rows, lanes = q.shape
    pages = hot.shape[0] // 2
    page_len = hot.shape[1]
    block = math.gcd(requests, 16)
    chunks = math.gcd(pages, 4)
    hot = hot.reshape(chunks, pages // chunks, 2, page_len, lanes)
    return pl.pallas_call(
        functools.partial(hot_kernel, factor=factor, block=block),
        out_shape=jax.ShapeDtypeStruct(q.shape, q.dtype),
        in_specs=[VMEM_SPEC] * 4,
        out_specs=VMEM_SPEC,
        compiler_params=pltpu.CompilerParams(vmem_limit_bytes=VMEM_LIMIT),
    )(q, mix, stat, hot)


def exchange(value):
    return lax.all_to_all(value, "group", split_axis=0, concat_axis=0, tiled=True)


def on_device(
    queries, fresh_kv, page_pool, context_len, page_holder, page_index, hot_owner, hot_pages
):
    requests, steps, local_heads, head_dim = queries.shape
    max_pages = page_holder.shape[1]
    groups = lax.axis_size("group")
    factor = math.log2(math.e) / math.sqrt(head_dim)
    q = queries.reshape(requests, steps * local_heads, head_dim)
    fresh = fresh_kv[:, :, 0].transpose(0, 2, 1, 3)
    pool = page_pool[:, 0]
    body = CAP * steps * local_heads
    dealt = exchange(deal(hot_pages, pool))
    asked, slots = ask(context_len, page_holder, page_index, q, groups, page_pool.shape[3])
    asked, dealt = lax.optimization_barrier((asked, dealt))
    share = lax.dynamic_index_in_dim(dealt, hot_owner[0], 0, keepdims=False)
    asked, share = lax.optimization_barrier((asked, share))
    hot = lax.all_gather(share, "group", axis=0, tiled=False)

    def attend(sent, pages, slots, q, fresh):
        sent = exchange(sent)
        table = sent[:, body : body + CAP, 0:2].astype(jnp.int32).reshape(-1)
        served = exchange(serve(table, sent, pages, factor))
        return merge(slots, q, fresh, served, factor, local_heads, max_pages)

    def nothing(sent, pages, slots, q, fresh):
        return (jnp.zeros(q.shape, jnp.float32),) * 2

    mix, stat = lax.cond(hot_owner[0] >= 0, attend, nothing, asked, pool, slots, q, fresh)
    attended = attend_hot(q, mix, stat, hot, factor)
    return attended.reshape(requests, steps, local_heads, head_dim)


def solution(mesh):
    placed = (
        P("group", None, "head", None),
        P("group", None, "head", None, None),
        P("group", "head", None, None, None),
        P("group"),
        P("group", None),
        P("group", None),
        P(),
        P(),
    )
    return jax.shard_map(
        on_device,
        mesh=mesh,
        in_specs=placed,
        out_specs=P("group", None, "head", None),
        check_vma=False,
    )
```
